512 devices in a mesh: seq: 32 (over z, core), head: 16 (over y, x).
Axes of the slice: x: 4, y: 4, z: 16, core: 2. Of those that a mesh axis runs over, the one named last changes fastest.
Arguments:
- queries: bfloat16 [8192, 32, 128], P('seq', 'head'), may hold values from -6 to 6
- raw_keys: bfloat16 [8192, 128], P('seq'), may hold values from -24 to 24
- values: bfloat16 [8192, 32, 128], P('seq', 'head'), may hold values from -6 to 6
- cotangent: bfloat16 [8192, 32, 128], P('seq', 'head'), may hold values from -6 to 6
Outputs:
- output: bfloat16 [8192, 32, 128], P('seq', 'head')
- grad_queries: bfloat16 [8192, 32, 128], P('seq', 'head')
- grad_keys: bfloat16 [8192, 128], P('seq')
- grad_values: bfloat16 [8192, 32, 128], P('seq', 'head')
The draws below stay inside these ranges and needn't reach their ends.
All inputs are finite; a program needn't handle non-finite values.
Results may differ from the reference program's by a relative error of at most 0.0038.
Values sent between devices are 32-bit elements; how exact they have to be, the bound alone decides.
No kernel may reach another device: no remote copies, remote signals or barrier semaphores. Data moves between devices by JAX's collectives and lax.ppermute only.
A program may use at most 64 MiB of HBM per device.

```python
import jax
import jax.numpy as jnp
from jax import lax

DK = 128
DV = 128
HEADS = 32
BLOCK = 128
LENGTH = 8192


def block_levels(stream_key, dims, cuts, least, largest):
    def one(dim, blocks):
        heights = jax.random.uniform(jax.random.fold_in(jax.random.fold_in(stream_key, 6), dim), (blocks,), jnp.float32, least / len(cuts), largest / len(cuts))
        return jnp.repeat(jnp.exp(heights), dims[dim] // blocks).reshape((-1,) + (1,) * (len(dims) - dim - 1))

    level = one(*cuts[0])
    for cut in cuts[1:]:
        level = level * one(*cut)
    return level


def normal_values(rng, dims, spread, most, shards=(), kind=jnp.bfloat16):
    loudness = block_levels(rng, dims, shards, -0.22, 0.18) if shards else 1.0
    drawn = jax.random.normal(rng, dims, jnp.float32) * spread * loudness
    return jnp.minimum(jnp.maximum(drawn, -most), most).astype(kind)


def setup_inputs(seed: int = 0) -> dict:
    keys = jax.random.split(jax.random.key(seed), 5)
    queries = normal_values(keys[0], (LENGTH, HEADS, DK), 1.0, 6.0, ((0, 32), (1, 16)))
    raw_keys = normal_values(keys[1], (LENGTH, DK), 4.0, 24.0, ((0, 32),))
    values = normal_values(keys[2], (LENGTH, HEADS, DV), 1.0, 6.0, ((0, 32), (1, 16)))
    cotangent = normal_values(keys[3], (LENGTH, HEADS, DV), 1.0, 6.0, ((0, 32), (1, 16)))
    return {"queries": queries, "raw_keys": raw_keys, "values": values, "cotangent": cotangent}


HIGHEST = lax.Precision.HIGHEST

def unit_rows(raw):
    squared = lax.optimization_barrier(jnp.sum(raw * raw, axis=-1, keepdims=True))
    return raw / jnp.sqrt(squared + 1e-06)

def advance_block(carried, block_query, block_key, block_value, places):
    block_len, head_count, key_width = block_query.shape
    value_width = block_value.shape[1] // head_count
    key_gram = jnp.dot(block_key, block_key.T, precision=HIGHEST)
    lower_mat = jnp.eye(block_len, dtype=jnp.float32) + 2.0 * jnp.tril(key_gram, -1)
    stacked = jnp.concatenate([block_key, 0.5 * block_value], axis=1)
    solved = lax.linalg.triangular_solve(lower_mat, stacked, left_side=True, lower=True, unit_diagonal=True)
    w_rows = solved[:, :key_width]
    u_rows = solved[:, key_width:] - jnp.dot(w_rows, carried, precision=HIGHEST)
    scores = jnp.tril(jnp.einsum('chk,tk->hct', block_query, block_key, precision=HIGHEST))
    result = jnp.einsum('chk,khv->chv', block_query, carried.reshape(key_width, head_count, value_width), precision=HIGHEST)
    result = result + 2.0 * jnp.einsum('hct,thv->chv', scores, u_rows.reshape(block_len, head_count, value_width), precision=HIGHEST)
    result = result / jnp.sqrt(places)[:, None, None]
    carried = carried + 2.0 * jnp.dot(block_key.T, u_rows, precision=HIGHEST)
    return (result, carried)

def reference(queries, raw_keys, values, cotangent):
    places = jnp.arange(LENGTH, dtype=jnp.float32) + 1.0
    num_blocks = LENGTH // BLOCK

    def forward(query_full, key_full, value_full):
        unit_keys = unit_rows(key_full)
        inputs = (query_full.reshape(num_blocks, BLOCK, HEADS, DK), unit_keys.reshape(num_blocks, BLOCK, DK), value_full.reshape(num_blocks, BLOCK, HEADS * DV), places.reshape(num_blocks, BLOCK))

        def advance(carried, block_in):
            result, carried_next = advance_block(carried, block_in[0], block_in[1], block_in[2], block_in[3])
            return (carried_next, result)
        start = jnp.zeros((DK, HEADS * DV), jnp.float32)
        final_state, results = lax.scan(jax.checkpoint(advance), start, inputs)
        return results.reshape(LENGTH, HEADS, DV)
    output, pull_back = jax.vjp(forward, queries.astype(jnp.float32), raw_keys.astype(jnp.float32), values.astype(jnp.float32))
    grad_query, grad_key, grad_value = pull_back(cotangent.astype(jnp.float32))
    return (output.astype(jnp.bfloat16), grad_query.astype(jnp.bfloat16), grad_key.astype(jnp.bfloat16), grad_value.astype(jnp.bfloat16))
```

```python
import functools

import jax
import jax.numpy as jnp
from jax import lax
from jax.experimental import pallas as pl
from jax.experimental.pallas import tpu as pltpu
from jax.sharding import PartitionSpec as P

T = 256
D = 128
F32 = jnp.float32
BF16 = jnp.bfloat16
VMEM_LIMIT = 48 * 1024 * 1024


def split(x):
    high = x.astype(BF16)
    return high, (x - high.astype(F32)).astype(BF16)


def exact(x):
    return x, None


def mm(a, b, over=(1, 0)):
    ca, cb = over
    terms = [(a[0], b[0])]
    if b[1] is not None:
        terms.append((a[0], b[1]))
    if a[1] is not None:
        terms.append((a[1], b[0]))
    left = jnp.concatenate([t[0] for t in terms], axis=ca)
    right = jnp.concatenate([t[1] for t in terms], axis=cb)
    return lax.dot_general(left, right, (((ca,), (cb,)), ((), ())), preferred_element_type=F32)


def iota(shape, dim):
    return lax.broadcasted_iota(jnp.int32, shape, dim)


def inverse(lower, size):
    row, col = iota((size, size), 0), iota((size, size), 1)
    level = row ^ col
    inv = jnp.where(row == col, 1.0, jnp.where((level == 1), -lower, 0.0))
    step = 2
    while step < size:
        part = jnp.where((level >= step) & (level < 2 * step), lower, 0.0)
        inv_pair = split(inv)
        inv = inv - mm(inv_pair, split(mm(split(part), inv_pair)))
        step *= 2
    return inv


def places_root(index):
    places = (index * T + iota((T, 1), 0) + 1).astype(F32)
    return 1.0 / jnp.sqrt(places)


def before_kernel(index_ref, raw_ref, q_ref, v_ref, d_ref, send_ref, k_ref, norm_ref, w_ref, m_ref, x_ref, z_ref,
                  qhat_ref, local_ref, qs_ref, vs_ref, ds_ref):
    qs_ref[...] = q_ref[...].astype(F32)
    vs_ref[...] = v_ref[...].astype(F32)
    ds_ref[...] = d_ref[...].astype(F32)
    rows = [pl.ds(head, T, stride=2) for head in range(2)]
    raw = raw_ref[...].astype(F32)
    norm = 1.0 / jnp.sqrt(jnp.sum(raw * raw, axis=1, keepdims=True) + 1e-06)
    key = raw * norm
    k_ref[...] = key
    norm_ref[...] = jnp.broadcast_to(norm, (T, D))
    root = places_root(index_ref[0])
    keys = split(key)
    gram = mm(keys, keys, (1, 1))
    row, col = iota((T, T), 0), iota((T, T), 1)
    lower = jnp.where(row > col, 2.0 * gram, 0.0)
    half = T // 2
    first = inverse(lower[:half, :half], half)
    second = inverse(lower[half:, half:], half)
    corner = -mm(split(second), split(mm(split(lower[half:, :half]), split(first))))
    inv = jnp.concatenate(
        [
            jnp.concatenate([first, jnp.zeros((half, half), F32)], axis=1),
            jnp.concatenate([corner, second], axis=1),
        ],
        axis=0,
    )
    invs = split(inv)
    w = 2.0 * mm(invs, keys)
    w_ref[...] = w
    ws = split(w)
    keys_t = split(key.T)
    eye = jnp.where(iota((D, D), 0) == iota((D, D), 1), 1.0, 0.0)
    send_ref[:, :D] = eye - mm(keys_t, ws)
    value = jnp.concatenate([vs_ref[r, :] for r in rows], axis=1).astype(BF16)
    x0 = mm(invs, exact(value))
    x_ref[...] = x0
    x0s = split(x0)
    send_ref[:, D : 3 * D] = mm(keys_t, x0s)
    inv_t = split(inv.T)
    m_ref[...] = mm(inv_t, keys)
    back = []
    for head in range(2):
        query = qs_ref[rows[head], :]
        grad = exact(ds_ref[rows[head], :].astype(BF16))
        score = jnp.where(row >= col, mm(exact(query.astype(BF16)), keys, (1, 1)), 0.0) * root
        scores = split(score)
        qhat = query * root - mm(scores, ws)
        qhat_ref[head] = qhat
        send_ref[:, (3 + head) * D : (4 + head) * D] = mm(split(qhat.T), grad)
        local_ref[head] = mm(scores, tuple(x[:, head * D : (head + 1) * D] for x in x0s))
        back.append(mm(split(score.T), grad))
    z_ref[...] = mm(inv_t, split(jnp.concatenate(back, axis=1)))


def pair_kernel(index_ref, got_ref, send_ref):
    core = index_ref[0] % 2
    at_b = pl.ds(pl.multiple_of(D + core * D, D), D)
    at_g = pl.ds(pl.multiple_of(3 * D + core * D, D), D)
    low, up = got_ref[0, :, :D], got_ref[1, :, :D]
    ahead = mm(split(up), split(jnp.concatenate([low, got_ref[0, :, at_b]], axis=1)))
    send_ref[:, :D] = ahead[:, :D]
    send_ref[:, D : 2 * D] = ahead[:, D:] + got_ref[1, :, at_b]
    send_ref[:, 2 * D :] = got_ref[0, :, at_g] + mm(split(low.T), split(got_ref[1, :, at_g]))


def level_kernel(first, last, bit, index_ref, got_ref, *refs):
    if first:
        send_ref, track_ref = refs
    else:
        old_ref, send_ref, track_ref = refs
    upper = (index_ref[0] // bit) % 2 == 1
    low, up = got_ref[0, :, :D], got_ref[1, :, :D]
    b_low, b_up = got_ref[0, :, D : 2 * D], got_ref[1, :, D : 2 * D]
    g_low, g_up = got_ref[0, :, 2 * D :], got_ref[1, :, 2 * D :]
    if last:
        top = (index_ref[0] // (2 * bit)) % 2 == 1
        step = mm(split(jnp.where(top, low.T, up)), split(jnp.where(top, g_up, b_low)))
        send_ref[...] = jnp.where(top, g_low, b_up) + step
    else:
        ahead = mm(split(up), split(jnp.concatenate([low, b_low], axis=1)))
        send_ref[:, :D] = ahead[:, :D]
        send_ref[:, D : 2 * D] = ahead[:, D:] + b_up
        send_ref[:, 2 * D :] = g_low + mm(split(low.T), split(g_up))
    other = jnp.where(upper, jnp.concatenate([low, b_low], axis=1), jnp.concatenate([up.T, g_up], axis=1))
    if first:
        eye = jnp.where(iota((D, D), 0) == iota((D, D), 1), 1.0, 0.0)
        blank = jnp.concatenate([eye, jnp.zeros((D, D), F32)], axis=1)
        track_ref[0] = jnp.where(upper, other, blank)
        track_ref[1] = jnp.where(upper, blank, other)
    else:
        mine = jnp.where(upper, old_ref[0], old_ref[1])
        new = mm(split(mine[:, :D]), split(other))
        new = jnp.concatenate([new[:, :D], new[:, D:] + mine[:, D:]], axis=1)
        track_ref[0] = jnp.where(upper, new, old_ref[0])
        track_ref[1] = jnp.where(upper, old_ref[1], new)


def top_kernel(bit, index_ref, got_ref, track_ref, send_ref):
    upper = (index_ref[0] // bit) % 2 == 1
    lead = jnp.where(upper, track_ref[0, :, :D], track_ref[1, :, :D])
    step = mm(split(lead), split(jnp.where(upper, got_ref[0], got_ref[1])))
    send_ref[:, :D] = track_ref[0, :, D:] + jnp.where(upper, step, 0.0)
    send_ref[:, D:] = track_ref[1, :, D:] + jnp.where(upper, 0.0, step)


def after_kernel(index_ref, pair_ref, got_ref, q_ref, d_ref, k_ref, w_ref, m_ref, x_ref, z_ref, qhat_ref, local_ref,
                 out_ref, gq_ref, gv_ref, gk_ref, qs_ref, ds_ref, os_ref, gs_ref, zs_ref):
    qs_ref[...] = q_ref[...].astype(F32)
    ds_ref[...] = d_ref[...].astype(F32)
    rows = [pl.ds(head, T, stride=2) for head in range(2)]
    upper = index_ref[0] % 2 == 1
    state = jnp.concatenate([got_ref[0, :, :D], got_ref[1, :, :D]], axis=1)
    adjoint = jnp.concatenate([got_ref[0, :, D:], got_ref[1, :, D:]], axis=1)
    step = mm(
        split(jnp.where(upper, pair_ref[0, :, :D], pair_ref[1, :, :D].T)),
        split(jnp.where(upper, state, adjoint)),
    )
    state = jnp.where(upper, step + pair_ref[0, :, D : 3 * D], state)
    adjoint = jnp.where(upper, adjoint, step + pair_ref[1, :, 3 * D :])
    states, adjoints = split(state), split(adjoint)
    root = places_root(index_ref[0])
    keys = split(k_ref[...])
    row, col = iota((T, T), 0), iota((T, T), 1)
    x = x_ref[...] - mm(split(w_ref[...]), states)
    xs = split(x)
    z = z_ref[...] + mm(split(m_ref[...]), adjoints)
    zs = split(z)
    edge = jnp.where(row > col, mm(zs, xs, (1, 1)), 0.0)
    gk = mm(xs, adjoints, (1, 1)) - 2.0 * mm(zs, states, (1, 1)) - 2.0 * mm(split(edge + edge.T), keys)
    for head in range(2):
        part = slice(head * D, (head + 1) * D)
        head_states = tuple(s[:, part] for s in states)
        query = exact(qs_ref[rows[head], :].astype(BF16))
        grad = exact(ds_ref[rows[head], :].astype(BF16))
        os_ref[rows[head], :] = local_ref[head] + mm(split(qhat_ref[head]), head_states)
        mix = jnp.where(row >= col, mm(grad, tuple(s[:, part] for s in xs), (1, 1)), 0.0) * root
        gs_ref[rows[head], :] = root * mm(grad, head_states, (1, 1)) + mm(split(mix), keys)
        gk = gk + mm(split(mix.T), query)
        zs_ref[rows[head], :] = z[:, part]
    gk_ref[...] = gk
    out_ref[...] = os_ref[...].astype(BF16)
    gq_ref[...] = gs_ref[...].astype(BF16)
    gv_ref[...] = zs_ref[...].astype(BF16)


def sum_kernel(got_ref, out_ref):
    out_ref[...] = jnp.broadcast_to(jnp.sum(got_ref[...], axis=0, keepdims=True), out_ref.shape)


def key_kernel(got_ref, k_ref, norm_ref, out_ref):
    total, key = got_ref[...], k_ref[...]
    along = jnp.sum(total * key, axis=1, keepdims=True)
    out_ref[...] = ((total - key * along) * norm_ref[...]).astype(BF16)


def call(kernel, outs, *operands, scratch=(), scalars=1):
    memory = [pl.BlockSpec(memory_space=pltpu.SMEM)] * scalars
    memory += [pl.BlockSpec(memory_space=pltpu.VMEM)] * (len(operands) - scalars)
    single = not isinstance(outs, list)
    shapes = [outs] if single else outs
    result = pl.pallas_call(
        kernel,
        out_shape=[jax.ShapeDtypeStruct(*s) for s in shapes],
        in_specs=memory,
        out_specs=[pl.BlockSpec(memory_space=pltpu.VMEM)] * len(shapes),
        scratch_shapes=list(scratch),
        compiler_params=pltpu.CompilerParams(vmem_limit_bytes=VMEM_LIMIT),
    )(*operands)
    return result[0] if single else result


def exchange(x, bit):
    size = lax.axis_size("seq")
    groups = [[i, i + bit] for i in range(size) if (i // bit) % 2 == 0]
    return lax.all_gather(x, "seq", axis_index_groups=groups)


def shards(queries, raw_keys, values, cotangent):
    index = lax.axis_index("seq").astype(jnp.int32).reshape(1)
    q = queries.reshape(2 * T, D)
    v = values.reshape(2 * T, D)
    d = cotangent.reshape(2 * T, D)
    wide = pltpu.VMEM((2 * T, D), F32)
    send, key, norm, w, m, x0, z0, qhat, local = call(
        before_kernel,
        [
            ((D, 5 * D), F32),
            ((T, D), F32),
            ((T, D), F32),
            ((T, D), F32),
            ((T, D), F32),
            ((T, 2 * D), F32),
            ((T, 2 * D), F32),
            ((2, T, D), F32),
            ((2, T, D), F32),
        ],
        index, raw_keys, q, v, d,
        scratch=[wide] * 3,
    )
    pair = exchange(send, 1)
    send = call(pair_kernel, ((D, 3 * D), F32), index, pair)
    size = lax.axis_size("seq")
    bit = 2
    track = None
    while bit < size // 2:
        got = exchange(send, bit)
        last = bit == size // 4
        send, track = call(
            functools.partial(level_kernel, track is None, last, bit),
            [((D, D if last else 3 * D), F32), ((2, D, 2 * D), F32)],
            index, got, *([] if track is None else [track]),
        )
        bit *= 2
    send = call(functools.partial(top_kernel, bit), ((D, 2 * D), F32), index, exchange(send, bit), track)
    got = exchange(send, 1)
    out, gq, gv, gk = call(
        after_kernel,
        [((2 * T, D), BF16), ((2 * T, D), BF16), ((2 * T, D), BF16), ((T, D), F32)],
        index, pair, got, q, d, key, w, m, x0, z0, qhat, local,
        scratch=[wide] * 5,
    )
    peers = lax.axis_size("head")
    pieces = lax.all_to_all(gk.reshape(peers, T // peers, D), "head", 0, 0)
    totals = call(sum_kernel, ((peers, T // peers, D), F32), pieces, scalars=0)
    total = lax.all_to_all(totals, "head", 0, 0).reshape(T, D)
    gkey = call(key_kernel, ((T, D), BF16), total, key, norm, scalars=0)
    shape = queries.shape
    return out.reshape(shape), gq.reshape(shape), gkey, gv.reshape(shape)


def solution(mesh):
    split_both = P("seq", "head", None)
    keys_only = P("seq", None)
    return jax.shard_map(
        shards,
        mesh=mesh,
        in_specs=(split_both, keys_only, split_both, split_both),
        out_specs=(split_both, split_both, keys_only, split_both),
        check_vma=False,
    )
```

```python
import functools

import jax
import jax.numpy as jnp
from jax import lax
from jax.experimental import pallas as pl
from jax.experimental.pallas import tpu as pltpu
from jax.sharding import PartitionSpec as P

T = 256
D = 128
C = D // 2
F32 = jnp.float32
BF16 = jnp.bfloat16
VMEM_LIMIT = 48 * 1024 * 1024
LONG = pl.CostEstimate(flops=4000000000, bytes_accessed=4000000, transcendentals=0)


def split(x):
    high = x.astype(BF16)
    return high, (x - high.astype(F32)).astype(BF16)


def exact(x):
    return x, None


def mm(a, b, over=(1, 0)):
    ca, cb = over
    terms = [(a[0], b[0])]
    if b[1] is not None:
        terms.append((a[0], b[1]))
    if a[1] is not None:
        terms.append((a[1], b[0]))
    left = jnp.concatenate([t[0] for t in terms], axis=ca)
    right = jnp.concatenate([t[1] for t in terms], axis=cb)
    return lax.dot_general(left, right, (((ca,), (cb,)), ((), ())), preferred_element_type=F32)


def iota(shape, dim):
    return lax.broadcasted_iota(jnp.int32, shape, dim)


def inverse(lower, size):
    row, col = iota((size, size), 0), iota((size, size), 1)
    level = row ^ col
    inv = jnp.where(row == col, 1.0, jnp.where((level == 1), -lower, 0.0))
    step = 2
    while step < size:
        part = jnp.where((level >= step) & (level < 2 * step), lower, 0.0)
        inv_pair = split(inv)
        inv = inv - mm(inv_pair, split(mm(split(part), inv_pair)))
        step *= 2
    return inv


def places_root(index):
    places = (index * T + iota((T, 1), 0) + 1).astype(F32)
    return 1.0 / jnp.sqrt(places)


def keys_kernel(raw_ref, k_ref, norm_ref, inv_ref):
    raw = raw_ref[...].astype(F32)
    norm = 1.0 / jnp.sqrt(jnp.sum(raw * raw, axis=1, keepdims=True) + 1e-06)
    key = raw * norm
    k_ref[...] = key
    norm_ref[...] = jnp.broadcast_to(norm, (T, D))
    keys = split(key)
    gram = mm(keys, keys, (1, 1))
    row, col = iota((T, T), 0), iota((T, T), 1)
    lower = jnp.where(row > col, 2.0 * gram, 0.0)
    half = T // 2
    first = inverse(lower[:half, :half], half)
    second = inverse(lower[half:, half:], half)
    corner = -mm(split(second), split(mm(split(lower[half:, :half]), split(first))))
    inv_ref[:half, :half] = first
    inv_ref[:half, half:] = jnp.zeros((half, half), F32)
    inv_ref[half:, :half] = corner
    inv_ref[half:, half:] = second


def before_kernel(index_ref, k_ref, inv_ref, q_ref, v_ref, d_ref, send_ref, w_ref, m_ref, x_ref, z_ref,
                  qs_ref, vs_ref, ds_ref):
    qs_ref[...] = q_ref[...].astype(F32)
    vs_ref[...] = v_ref[...].astype(F32)
    ds_ref[...] = d_ref[...].astype(F32)
    rows = [pl.ds(head, T, stride=2) for head in range(2)]
    root = places_root(index_ref[0])
    row, col = iota((T, T), 0), iota((T, T), 1)
    key, inv = k_ref[...], inv_ref[...]
    keys, invs = split(key), split(inv)
    w = 2.0 * mm(invs, keys)
    w_ref[...] = w
    ws = split(w)
    keys_t = split(key.T)
    eye = jnp.where(iota((D, D), 0) == iota((D, D), 1), 1.0, 0.0)
    send_ref[:, :D] = eye - mm(keys_t, ws)
    value = jnp.concatenate([vs_ref[r, :] for r in rows], axis=1).astype(BF16)
    x0 = mm(invs, exact(value))
    x_ref[...] = x0
    send_ref[:, D : 3 * D] = mm(keys_t, split(x0))
    inv_t = split(inv.T)
    m_ref[...] = mm(inv_t, keys)
    back = []
    for head in range(2):
        query = qs_ref[rows[head], :]
        grad = exact(ds_ref[rows[head], :].astype(BF16))
        score = jnp.where(row >= col, mm(exact(query.astype(BF16)), keys, (1, 1)), 0.0) * root
        qhat = query * root - mm(split(score), ws)
        send_ref[:, (3 + head) * D : (4 + head) * D] = mm(split(qhat.T), grad)
        back.append(mm(split(score.T), grad))
    z_ref[...] = mm(inv_t, split(jnp.concatenate(back, axis=1)))


def pair_kernel(index_ref, got_ref, send_ref):
    core = index_ref[0] % 2
    at_b = pl.ds(pl.multiple_of(D + core * D, D), D)
    at_g = pl.ds(pl.multiple_of(3 * D + core * D, D), D)
    low, up = got_ref[0, :, :D], got_ref[1, :, :D]
    ahead = mm(split(up), split(jnp.concatenate([low, got_ref[0, :, at_b]], axis=1)))
    send_ref[:, :D] = ahead[:, :D]
    send_ref[:, D : 2 * D] = ahead[:, D:] + got_ref[1, :, at_b]
    send_ref[:, 2 * D :] = got_ref[0, :, at_g] + mm(split(low.T), split(got_ref[1, :, at_g]))


def chip_kernel(index_ref, got_ref, send_ref):
    right = (index_ref[0] // 2) % 2 == 1
    low, up = got_ref[0, :, :D], got_ref[1, :, :D]
    b_low, b_up, g_low, g_up = pick(got_ref, right)
    ahead = mm(split(up), split(jnp.concatenate([low, b_low], axis=1)))
    send_ref[:, :D] = ahead[:, :D]
    send_ref[:, D:] = jnp.concatenate(
        [ahead[:, D:] + b_up, g_low + mm(split(low.T), split(g_up))], axis=1
    )


def pick(got_ref, right):
    return [
        jnp.where(right, half[:, C:], half[:, :C])
        for half in (
            got_ref[0, :, D : 2 * D], got_ref[1, :, D : 2 * D], got_ref[0, :, 2 * D :], got_ref[1, :, 2 * D :]
        )
    ]


def level_kernel(first, last, bit, index_ref, got_ref, *refs):
    if first:
        send_ref, track_ref = refs
    else:
        old_ref, send_ref, track_ref = refs
    upper = (index_ref[0] // bit) % 2 == 1
    low, up = got_ref[0, :, :D], got_ref[1, :, :D]
    b_low, b_up = got_ref[0, :, D : D + C], got_ref[1, :, D : D + C]
    g_low, g_up = got_ref[0, :, D + C :], got_ref[1, :, D + C :]
    if last:
        top = (index_ref[0] // (2 * bit)) % 2 == 1
        step = mm(split(jnp.where(top, low.T, up)), split(jnp.where(top, g_up, b_low)))
        half = jnp.where(top, g_low, b_up) + step
        send_ref[...] = jnp.concatenate([half[:C], half[C:]], axis=1)
    else:
        ahead = mm(split(up), split(jnp.concatenate([low, b_low], axis=1)))
        send_ref[:, :D] = ahead[:, :D]
        send_ref[:, D:] = jnp.concatenate(
            [ahead[:, D:] + b_up, g_low + mm(split(low.T), split(g_up))], axis=1
        )
    other = jnp.where(upper, jnp.concatenate([low, b_low], axis=1), jnp.concatenate([up.T, g_up], axis=1))
    if first:
        eye = jnp.where(iota((D, D), 0) == iota((D, D), 1), 1.0, 0.0)
        blank = jnp.concatenate([eye, jnp.zeros((D, C), F32)], axis=1)
        track_ref[0] = jnp.where(upper, other, blank)
        track_ref[1] = jnp.where(upper, blank, other)
    else:
        mine = jnp.where(upper, old_ref[0], old_ref[1])
        new = mm(split(mine[:, :D]), split(other))
        new = jnp.concatenate([new[:, :D], new[:, D:] + mine[:, D:]], axis=1)
        track_ref[0] = jnp.where(upper, new, old_ref[0])
        track_ref[1] = jnp.where(upper, old_ref[1], new)


def top_kernel(bit, index_ref, got_ref, track_ref, chips_ref, send_ref):
    upper = (index_ref[0] // bit) % 2 == 1
    lead = jnp.where(upper, track_ref[0, :, :D], track_ref[1, :, :D])
    got = jnp.where(upper, got_ref[0], got_ref[1])
    step = mm(split(lead), split(jnp.concatenate([got[:, :C], got[:, C:]], axis=0)))
    state = track_ref[0, :, D:] + jnp.where(upper, step, 0.0)
    adjoint = track_ref[1, :, D:] + jnp.where(upper, 0.0, step)
    b_low, _, _, g_up = pick(chips_ref, (index_ref[0] // 2) % 2 == 1)
    later = b_low + mm(split(chips_ref[0, :, :D]), split(state))
    sooner = g_up + mm(split(chips_ref[1, :, :D].T), split(adjoint))
    send_ref[:, :D] = jnp.concatenate([state, later], axis=1)
    send_ref[:, D:] = jnp.concatenate([sooner, adjoint], axis=1)


def after_kernel(index_ref, pair_ref, got_ref, q_ref, d_ref, k_ref, w_ref, m_ref, x0_ref, z0_ref,
                 gk_ref, s_ref, x_ref, z_ref, qs_ref, ds_ref):
    qs_ref[...] = q_ref[...].astype(F32)
    ds_ref[...] = d_ref[...].astype(F32)
    rows = [pl.ds(head, T, stride=2) for head in range(2)]
    upper = index_ref[0] % 2 == 1
    chip = (index_ref[0] // 2) % 2 == 1
    order = (0, 2, 1, 3)
    both = [jnp.concatenate([got_ref[j, :, half * D : (half + 1) * D] for j in order], axis=1) for half in range(2)]
    both = [
        [jnp.concatenate([b[:, (2 * i + w) * C : (2 * i + w + 1) * C] for i in range(4)], axis=1) for w in range(2)]
        for b in both
    ]
    state, adjoint = (jnp.where(chip, b[1], b[0]) for b in both)
    step = mm(
        split(jnp.where(upper, pair_ref[0, :, :D], pair_ref[1, :, :D].T)),
        split(jnp.where(upper, state, adjoint)),
    )
    state = jnp.where(upper, step + pair_ref[0, :, D : 3 * D], state)
    adjoint = jnp.where(upper, adjoint, step + pair_ref[1, :, 3 * D :])
    s_ref[...] = state
    states, adjoints = split(state), split(adjoint)
    root = places_root(index_ref[0])
    keys = split(k_ref[...])
    row, col = iota((T, T), 0), iota((T, T), 1)
    x = x0_ref[...] - mm(split(w_ref[...]), states)
    x_ref[...] = x
    xs = split(x)
    z = z0_ref[...] + mm(split(m_ref[...]), adjoints)
    z_ref[...] = z
    zs = split(z)
    edge = jnp.where(row > col, mm(zs, xs, (1, 1)), 0.0)
    gk = mm(xs, adjoints, (1, 1)) - 2.0 * mm(zs, states, (1, 1)) - 2.0 * mm(split(edge + edge.T), keys)
    for head in range(2):
        part = slice(head * D, (head + 1) * D)
        query = exact(qs_ref[rows[head], :].astype(BF16))
        grad = exact(ds_ref[rows[head], :].astype(BF16))
        mix = jnp.where(row >= col, mm(grad, tuple(s[:, part] for s in xs), (1, 1)), 0.0) * root
        gk = gk + mm(split(mix.T), query)
    gk_ref[...] = gk


def rest_kernel(index_ref, q_ref, d_ref, k_ref, s_ref, x_ref, z_ref, out_ref, gq_ref, gv_ref, qs_ref, ds_ref,
                os_ref, gs_ref, zs_ref):
    qs_ref[...] = q_ref[...].astype(F32)
    ds_ref[...] = d_ref[...].astype(F32)
    rows = [pl.ds(head, T, stride=2) for head in range(2)]
    root = places_root(index_ref[0])
    keys = split(k_ref[...])
    row, col = iota((T, T), 0), iota((T, T), 1)
    states, xs = split(s_ref[...]), split(x_ref[...])
    for head in range(2):
        part = slice(head * D, (head + 1) * D)
        head_states, head_xs = tuple(s[:, part] for s in states), tuple(s[:, part] for s in xs)
        query = exact(qs_ref[rows[head], :].astype(BF16))
        grad = exact(ds_ref[rows[head], :].astype(BF16))
        score = jnp.where(row >= col, mm(query, keys, (1, 1)), 0.0)
        os_ref[rows[head], :] = root * (mm(query, head_states) + mm(split(score), head_xs))
        mix = jnp.where(row >= col, mm(grad, head_xs, (1, 1)), 0.0)
        gs_ref[rows[head], :] = root * (mm(grad, head_states, (1, 1)) + mm(split(mix), keys))
        zs_ref[rows[head], :] = z_ref[:, part]
    out_ref[...] = os_ref[...].astype(BF16)
    gq_ref[...] = gs_ref[...].astype(BF16)
    gv_ref[...] = zs_ref[...].astype(BF16)


def sum_kernel(got_ref, out_ref):
    out_ref[...] = jnp.broadcast_to(jnp.sum(got_ref[...], axis=0, keepdims=True), out_ref.shape)


def key_kernel(got_ref, k_ref, norm_ref, out_ref):
    total, key = got_ref[...], k_ref[...]
    along = jnp.sum(total * key, axis=1, keepdims=True)
    out_ref[...] = ((total - key * along) * norm_ref[...]).astype(BF16)


def call(kernel, outs, *operands, scratch=(), scalars=1, cost=None):
    spaces = [pltpu.SMEM] * scalars + [pltpu.VMEM] * (len(operands) - scalars)
    single = not isinstance(outs, list)
    shapes = [outs] if single else outs
    result = pl.pallas_call(
        kernel,
        out_shape=[jax.ShapeDtypeStruct(*s) for s in shapes],
        in_specs=[pl.BlockSpec(memory_space=space) for space in spaces],
        out_specs=[pl.BlockSpec(memory_space=pltpu.VMEM)] * len(shapes),
        scratch_shapes=list(scratch),
        compiler_params=pltpu.CompilerParams(vmem_limit_bytes=VMEM_LIMIT),
        cost_estimate=cost,
    )(*operands)
    return result[0] if single else result


def exchange(x, bits):
    size = lax.axis_size("seq")
    mask = sum(bits)
    offsets = [0]
    for bit in bits:
        offsets = offsets + [o + bit for o in offsets]
    groups = [[i + o for o in offsets] for i in range(size) if i & mask == 0]
    return lax.all_gather(x, "seq", axis_index_groups=groups)


def shards(queries, raw_keys, values, cotangent):
    index = lax.axis_index("seq").astype(jnp.int32).reshape(1)
    q = queries.reshape(2 * T, D)
    v = values.reshape(2 * T, D)
    d = cotangent.reshape(2 * T, D)
    wide = pltpu.VMEM((2 * T, D), F32)
    key, norm, inv = call(
        keys_kernel, [((T, D), F32), ((T, D), F32), ((T, T), F32)], raw_keys, scalars=0, cost=LONG
    )
    send, w, m, x0, z0 = call(
        before_kernel,
        [((D, 5 * D), F32), ((T, D), F32), ((T, D), F32), ((T, 2 * D), F32), ((T, 2 * D), F32)],
        index, key, inv, q, v, d,
        scratch=[wide] * 3,
    )
    pair = exchange(send, (1,))
    send = call(pair_kernel, ((D, 3 * D), F32), index, pair)
    chips = exchange(send, (2,))
    send = call(chip_kernel, ((D, 2 * D), F32), index, chips)
    size = lax.axis_size("seq")
    bit = 4
    track = None
    while bit < size // 2:
        got = exchange(send, (bit,))
        last = bit == size // 4
        send, track = call(
            functools.partial(level_kernel, track is None, last, bit),
            [((C, D) if last else (D, 2 * D), F32), ((2, D, D + C), F32)],
            index, got, *([] if track is None else [track]),
        )
        bit *= 2
    send = call(functools.partial(top_kernel, bit), ((D, 2 * D), F32), index, exchange(send, (bit,)), track, chips)
    got = exchange(send, (1, 2))
    gk, state, x, z = call(
        after_kernel,
        [((T, D), F32), ((D, 2 * D), F32), ((T, 2 * D), F32), ((T, 2 * D), F32)],
        index, pair, got, q, d, key, w, m, x0, z0,
        scratch=[wide] * 2,
    )
    peers = lax.axis_size("head")
    pieces = lax.all_to_all(gk.reshape(peers, T // peers, D), "head", 0, 0)
    out, gq, gv = call(
        rest_kernel,
        [((2 * T, D), BF16)] * 3,
        index, q, d, key, state, x, z,
        scratch=[wide] * 5,
        cost=LONG,
    )
    totals = call(sum_kernel, ((peers, T // peers, D), F32), pieces, scalars=0)
    total = lax.all_to_all(totals, "head", 0, 0).reshape(T, D)
    gkey = call(key_kernel, ((T, D), BF16), total, key, norm, scalars=0)
    shape = queries.shape
    return out.reshape(shape), gq.reshape(shape), gkey, gv.reshape(shape)


def solution(mesh):
    split_both = P("seq", "head", None)
    keys_only = P("seq", None)
    return jax.shard_map(
        shards,
        mesh=mesh,
        in_specs=(split_both, keys_only, split_both, split_both),
        out_specs=(split_both, split_both, keys_only, split_both),
        check_vma=False,
    )
```

```python
import functools

import jax
import jax.numpy as jnp
from jax import lax
from jax.experimental import pallas as pl
from jax.experimental.pallas import tpu as pltpu
from jax.sharding import PartitionSpec as P

T = 256
PARTS = 32
D = 128
C = D // 2
F32 = jnp.float32
BF16 = jnp.bfloat16
VMEM_LIMIT = 48 * 1024 * 1024
LONG = pl.CostEstimate(flops=4000000000, bytes_accessed=4000000, transcendentals=0)


def split(x):
    high = x.astype(BF16)
    return high, (x - high.astype(F32)).astype(BF16)


def exact(x):
    return x, None


def mm(a, b, over=(1, 0)):
    ca, cb = over
    terms = [(a[0], b[0])]
    if b[1] is not None:
        terms.append((a[0], b[1]))
    if a[1] is not None:
        terms.append((a[1], b[0]))
    left = jnp.concatenate([t[0] for t in terms], axis=ca)
    right = jnp.concatenate([t[1] for t in terms], axis=cb)
    return lax.dot_general(left, right, (((ca,), (cb,)), ((), ())), preferred_element_type=F32)


def iota(shape, dim):
    return lax.broadcasted_iota(jnp.int32, shape, dim)


def inverse(lower, size):
    row, col = iota((size, size), 0), iota((size, size), 1)
    level = row ^ col
    inv = jnp.where(row == col, 1.0, jnp.where((level == 1), -lower, 0.0))
    step = 2
    while step < size:
        part = jnp.where((level >= step) & (level < 2 * step), lower, 0.0)
        inv_pair = split(inv)
        inv = inv - mm(inv_pair, split(mm(split(part), inv_pair)))
        step *= 2
    return inv


def places_root(index):
    places = (index * T + iota((T, 1), 0) + 1).astype(F32)
    return 1.0 / jnp.sqrt(places)


def keys_kernel(raw_ref, k_ref, norm_ref, inv_ref):
    raw = raw_ref[...].astype(F32)
    norm = 1.0 / jnp.sqrt(jnp.sum(raw * raw, axis=1, keepdims=True) + 1e-06)
    key = raw * norm
    k_ref[...] = key
    norm_ref[...] = jnp.broadcast_to(norm, (T, D))
    keys = split(key)
    gram = mm(keys, keys, (1, 1))
    row, col = iota((T, T), 0), iota((T, T), 1)
    lower = jnp.where(row > col, 2.0 * gram, 0.0)
    half = T // 2
    first = inverse(lower[:half, :half], half)
    second = inverse(lower[half:, half:], half)
    corner = -mm(split(second), split(mm(split(lower[half:, :half]), split(first))))
    inv_ref[:half, :half] = first
    inv_ref[:half, half:] = jnp.zeros((half, half), F32)
    inv_ref[half:, :half] = corner
    inv_ref[half:, half:] = second


def before_kernel(index_ref, k_ref, inv_ref, q_ref, v_ref, d_ref, send_ref, w_ref, m_ref, x_ref, z_ref,
                  qs_ref, vs_ref, ds_ref):
    qs_ref[...] = q_ref[...].astype(F32)
    vs_ref[...] = v_ref[...].astype(F32)
    ds_ref[...] = d_ref[...].astype(F32)
    rows = [pl.ds(head, T, stride=2) for head in range(2)]
    root = places_root(index_ref[0])
    row, col = iota((T, T), 0), iota((T, T), 1)
    key, inv = k_ref[...], inv_ref[...]
    keys, invs = split(key), split(inv)
    w = 2.0 * mm(invs, keys)
    w_ref[...] = w
    ws = split(w)
    keys_t = split(key.T)
    eye = jnp.where(iota((D, D), 0) == iota((D, D), 1), 1.0, 0.0)
    send_ref[:, :D] = eye - mm(keys_t, ws)
    value = jnp.concatenate([vs_ref[r, :] for r in rows], axis=1).astype(BF16)
    x0 = mm(invs, exact(value))
    x_ref[...] = x0
    send_ref[:, D : 3 * D] = mm(keys_t, split(x0))
    inv_t = split(inv.T)
    m_ref[...] = mm(inv_t, keys)
    back = []
    for head in range(2):
        query = qs_ref[rows[head], :]
        grad = exact(ds_ref[rows[head], :].astype(BF16))
        score = jnp.where(row >= col, mm(exact(query.astype(BF16)), keys, (1, 1)), 0.0) * root
        qhat = query * root - mm(split(score), ws)
        send_ref[:, (3 + head) * D : (4 + head) * D] = mm(split(qhat.T), grad)
        back.append(mm(split(score.T), grad))
    z_ref[...] = mm(inv_t, split(jnp.concatenate(back, axis=1)))


def pair_kernel(index_ref, got_ref, send_ref):
    core = index_ref[0] % 2
    at_b = pl.ds(pl.multiple_of(D + core * D, D), D)
    at_g = pl.ds(pl.multiple_of(3 * D + core * D, D), D)
    low, up = got_ref[0, :, :D], got_ref[1, :, :D]
    ahead = mm(split(up), split(jnp.concatenate([low, got_ref[0, :, at_b]], axis=1)))
    send_ref[:, :D] = ahead[:, :D]
    send_ref[:, D : 2 * D] = ahead[:, D:] + got_ref[1, :, at_b]
    send_ref[:, 2 * D :] = got_ref[0, :, at_g] + mm(split(low.T), split(got_ref[1, :, at_g]))


def chip_kernel(index_ref, got_ref, send_ref):
    right = (index_ref[0] // 2) % 2 == 1
    low, up = got_ref[0, :, :D], got_ref[1, :, :D]
    b_low, b_up, g_low, g_up = pick(got_ref, right)
    ahead = mm(split(up), split(jnp.concatenate([low, b_low], axis=1)))
    send_ref[:, :D] = ahead[:, :D]
    send_ref[:, D:] = jnp.concatenate(
        [ahead[:, D:] + b_up, g_low + mm(split(low.T), split(g_up))], axis=1
    )


def pick(got_ref, right):
    return [
        jnp.where(right, half[:, C:], half[:, :C])
        for half in (
            got_ref[0, :, D : 2 * D], got_ref[1, :, D : 2 * D], got_ref[0, :, 2 * D :], got_ref[1, :, 2 * D :]
        )
    ]


def pack(x):
    return jnp.concatenate([x[:C], x[C:]], axis=1)


def unpack(x):
    return jnp.concatenate([x[:, :C], x[:, C:]], axis=0)


def block_kernel(index_ref, got_ref, send_ref, block_ref, track_ref):
    block = index_ref[0] // 8
    upper = (index_ref[0] // 4) % 2 == 1
    low, up = got_ref[0, :, :D], got_ref[1, :, :D]
    b_low, b_up = got_ref[0, :, D : D + C], got_ref[1, :, D : D + C]
    g_low, g_up = got_ref[0, :, D + C :], got_ref[1, :, D + C :]
    ahead = mm(split(up), split(jnp.concatenate([low, b_low], axis=1)))
    b_all = ahead[:, D:] + b_up
    g_all = g_low + mm(split(low.T), split(g_up))
    send_ref[...] = pack(jnp.where(block == 3, g_all, b_all))
    block_ref[:, :D] = ahead[:, :D]
    block_ref[:, D:] = jnp.concatenate([b_all, g_all], axis=1)
    eye = jnp.where(iota((D, D), 0) == iota((D, D), 1), 1.0, 0.0)
    blank = jnp.concatenate([eye, jnp.zeros((D, C), F32)], axis=1)
    track_ref[0] = jnp.where(upper, jnp.concatenate([low, b_low], axis=1), blank)
    track_ref[1] = jnp.where(upper, blank, jnp.concatenate([up.T, g_up], axis=1))


def hop_kernel(downward, index_ref, got_ref, block_ref, send_ref):
    down = index_ref[0] // 8 == downward
    whole = block_ref[:, :D]
    got = unpack(jnp.where(down, got_ref[1], got_ref[0]))
    own = jnp.where(down, block_ref[:, D + C :], block_ref[:, D : D + C])
    send_ref[...] = pack(own + mm(split(jnp.where(down, whole.T, whole)), split(got)))


def top_kernel(index_ref, first_ref, second_ref, third_ref, track_ref, chips_ref, send_ref):
    block = index_ref[0] // 8
    got = jnp.where(
        block == 1, first_ref[0], jnp.where(block == 2, second_ref[0], jnp.where(block == 3, third_ref[0], 0.0))
    )
    state = track_ref[0, :, D:] + mm(split(track_ref[0, :, :D]), split(unpack(got)))
    got = jnp.where(
        block == 2, first_ref[1], jnp.where(block == 1, second_ref[1], jnp.where(block == 0, third_ref[1], 0.0))
    )
    adjoint = track_ref[1, :, D:] + mm(split(track_ref[1, :, :D]), split(unpack(got)))
    b_low, _, _, g_up = pick(chips_ref, (index_ref[0] // 2) % 2 == 1)
    later = b_low + mm(split(chips_ref[0, :, :D]), split(state))
    sooner = g_up + mm(split(chips_ref[1, :, :D].T), split(adjoint))
    send_ref[:, :D] = jnp.concatenate([state, later], axis=1)
    send_ref[:, D:] = jnp.concatenate([sooner, adjoint], axis=1)


def after_kernel(index_ref, pair_ref, got_ref, q_ref, d_ref, k_ref, w_ref, m_ref, x0_ref, z0_ref,
                 gk_ref, s_ref, x_ref, z_ref, qs_ref, ds_ref):
    qs_ref[...] = q_ref[...].astype(F32)
    ds_ref[...] = d_ref[...].astype(F32)
    rows = [pl.ds(head, T, stride=2) for head in range(2)]
    upper = index_ref[0] % 2 == 1
    chip = (index_ref[0] // 2) % 2 == 1
    order = (0, 2, 1, 3)
    both = [jnp.concatenate([got_ref[j, :, half * D : (half + 1) * D] for j in order], axis=1) for half in range(2)]
    both = [
        [jnp.concatenate([b[:, (2 * i + w) * C : (2 * i + w + 1) * C] for i in range(4)], axis=1) for w in range(2)]
        for b in both
    ]
    state, adjoint = (jnp.where(chip, b[1], b[0]) for b in both)
    step = mm(
        split(jnp.where(upper, pair_ref[0, :, :D], pair_ref[1, :, :D].T)),
        split(jnp.where(upper, state, adjoint)),
    )
    state = jnp.where(upper, step + pair_ref[0, :, D : 3 * D], state)
    adjoint = jnp.where(upper, adjoint, step + pair_ref[1, :, 3 * D :])
    s_ref[...] = state
    states, adjoints = split(state), split(adjoint)
    root = places_root(index_ref[0])
    keys = split(k_ref[...])
    row, col = iota((T, T), 0), iota((T, T), 1)
    x = x0_ref[...] - mm(split(w_ref[...]), states)
    x_ref[...] = x
    xs = split(x)
    z = z0_ref[...] + mm(split(m_ref[...]), adjoints)
    z_ref[...] = z
    zs = split(z)
    edge = jnp.where(row > col, mm(zs, xs, (1, 1)), 0.0)
    gk = mm(xs, adjoints, (1, 1)) - 2.0 * mm(zs, states, (1, 1)) - 2.0 * mm(split(edge + edge.T), keys)
    for head in range(2):
        part = slice(head * D, (head + 1) * D)
        query = exact(qs_ref[rows[head], :].astype(BF16))
        grad = exact(ds_ref[rows[head], :].astype(BF16))
        mix = jnp.where(row >= col, mm(grad, tuple(s[:, part] for s in xs), (1, 1)), 0.0) * root
        gk = gk + mm(split(mix.T), query)
    gk_ref[...] = gk


def rest_kernel(index_ref, q_ref, d_ref, k_ref, s_ref, x_ref, z_ref, out_ref, gq_ref, gv_ref, qs_ref, ds_ref,
                os_ref, gs_ref, zs_ref):
    qs_ref[...] = q_ref[...].astype(F32)
    ds_ref[...] = d_ref[...].astype(F32)
    rows = [pl.ds(head, T, stride=2) for head in range(2)]
    root = places_root(index_ref[0])
    keys = split(k_ref[...])
    row, col = iota((T, T), 0), iota((T, T), 1)
    states, xs = split(s_ref[...]), split(x_ref[...])
    for head in range(2):
        part = slice(head * D, (head + 1) * D)
        head_states, head_xs = tuple(s[:, part] for s in states), tuple(s[:, part] for s in xs)
        query = exact(qs_ref[rows[head], :].astype(BF16))
        grad = exact(ds_ref[rows[head], :].astype(BF16))
        score = jnp.where(row >= col, mm(query, keys, (1, 1)), 0.0)
        os_ref[rows[head], :] = root * (mm(query, head_states) + mm(split(score), head_xs))
        mix = jnp.where(row >= col, mm(grad, head_xs, (1, 1)), 0.0)
        gs_ref[rows[head], :] = root * (mm(grad, head_states, (1, 1)) + mm(split(mix), keys))
        zs_ref[rows[head], :] = z_ref[:, part]
    out_ref[...] = os_ref[...].astype(BF16)
    gq_ref[...] = gs_ref[...].astype(BF16)
    gv_ref[...] = zs_ref[...].astype(BF16)


def sum_kernel(got_ref, out_ref):
    out_ref[...] = jnp.broadcast_to(jnp.sum(got_ref[...], axis=0, keepdims=True), out_ref.shape)


def key_kernel(got_ref, k_ref, norm_ref, out_ref):
    total, key = got_ref[...], k_ref[...]
    along = jnp.sum(total * key, axis=1, keepdims=True)
    out_ref[...] = ((total - key * along) * norm_ref[...]).astype(BF16)


def call(kernel, outs, *operands, scratch=(), scalars=1, cost=None):
    spaces = [pltpu.SMEM] * scalars + [pltpu.VMEM] * (len(operands) - scalars)
    single = not isinstance(outs, list)
    shapes = [outs] if single else outs
    result = pl.pallas_call(
        kernel,
        out_shape=[jax.ShapeDtypeStruct(*s) for s in shapes],
        in_specs=[pl.BlockSpec(memory_space=space) for space in spaces],
        out_specs=[pl.BlockSpec(memory_space=pltpu.VMEM)] * len(shapes),
        scratch_shapes=list(scratch),
        compiler_params=pltpu.CompilerParams(vmem_limit_bytes=VMEM_LIMIT),
        cost_estimate=cost,
    )(*operands)
    return result[0] if single else result


def exchange(x, groups):
    return lax.all_gather(x, "seq", axis_index_groups=groups)


def near(*offsets):
    groups, taken = [], set()
    for i in range(PARTS):
        if i not in taken:
            groups.append([i + offset for offset in offsets])
            taken.update(groups[-1])
    return groups


CROSS = [[i, i + 24] for i in range(8)] + [[i, i + 8] for i in range(8, 16)]


def shards(queries, raw_keys, values, cotangent):
    index = lax.axis_index("seq").astype(jnp.int32).reshape(1)
    q = queries.reshape(2 * T, D)
    v = values.reshape(2 * T, D)
    d = cotangent.reshape(2 * T, D)
    wide = pltpu.VMEM((2 * T, D), F32)
    key, norm, inv = call(
        keys_kernel, [((T, D), F32), ((T, D), F32), ((T, T), F32)], raw_keys, scalars=0, cost=LONG
    )
    send, w, m, x0, z0 = call(
        before_kernel,
        [((D, 5 * D), F32), ((T, D), F32), ((T, D), F32), ((T, 2 * D), F32), ((T, 2 * D), F32)],
        index, key, inv, q, v, d,
        scratch=[wide] * 3,
    )
    pair = exchange(send, near(0, 1))
    send = call(pair_kernel, ((D, 3 * D), F32), index, pair)
    chips = exchange(send, near(0, 2))
    send = call(chip_kernel, ((D, 2 * D), F32), index, chips)
    send, block, track = call(
        block_kernel,
        [((C, D), F32), ((D, 2 * D), F32), ((2, D, D + C), F32)],
        index, exchange(send, near(0, 4)),
    )
    first = exchange(send, near(0, 8))
    send = call(functools.partial(hop_kernel, 2), ((C, D), F32), index, first, block)
    second = exchange(send, CROSS)
    send = call(functools.partial(hop_kernel, 1), ((C, D), F32), index, second, block)
    third = exchange(send, near(0, 8))
    send = call(top_kernel, ((D, 2 * D), F32), index, first, second, third, track, chips)
    got = exchange(send, near(0, 1, 2, 3))
    gk, state, x, z = call(
        after_kernel,
        [((T, D), F32), ((D, 2 * D), F32), ((T, 2 * D), F32), ((T, 2 * D), F32)],
        index, pair, got, q, d, key, w, m, x0, z0,
        scratch=[wide] * 2,
    )
    peers = lax.axis_size("head")
    pieces = lax.all_to_all(gk.reshape(peers, T // peers, D), "head", 0, 0)
    out, gq, gv = call(
        rest_kernel,
        [((2 * T, D), BF16)] * 3,
        index, q, d, key, state, x, z,
        scratch=[wide] * 5,
        cost=LONG,
    )
    totals = call(sum_kernel, ((peers, T // peers, D), F32), pieces, scalars=0)
    total = lax.all_to_all(totals, "head", 0, 0).reshape(T, D)
    gkey = call(key_kernel, ((T, D), BF16), total, key, norm, scalars=0)
    shape = queries.shape
    return out.reshape(shape), gq.reshape(shape), gkey, gv.reshape(shape)


def solution(mesh):
    split_both = P("seq", "head", None)
    keys_only = P("seq", None)
    return jax.shard_map(
        shards,
        mesh=mesh,
        in_specs=(split_both, keys_only, split_both, split_both),
        out_specs=(split_both, split_both, keys_only, split_both),
        check_vma=False,
    )
```

```python
import functools

import jax
import jax.numpy as jnp
from jax import lax
from jax.experimental import pallas as pl
from jax.experimental.pallas import tpu as pltpu
from jax.sharding import PartitionSpec as P

T = 256
PARTS = 32
D = 128
F32 = jnp.float32
BF16 = jnp.bfloat16
VMEM_LIMIT = 48 * 1024 * 1024
SHORT = pl.CostEstimate(flops=500000000, bytes_accessed=1000000, transcendentals=0)
LONG = pl.CostEstimate(flops=4000000000, bytes_accessed=4000000, transcendentals=0)


def split(x):
    high = x.astype(BF16)
    return high, (x - high.astype(F32)).astype(BF16)


def exact(x):
    return x, None


def mm(a, b, over=(1, 0)):
    ca, cb = over
    terms = [(a[0], b[0])]
    if b[1] is not None:
        terms.append((a[0], b[1]))
    if a[1] is not None:
        terms.append((a[1], b[0]))
    left = jnp.concatenate([t[0] for t in terms], axis=ca)
    right = jnp.concatenate([t[1] for t in terms], axis=cb)
    return lax.dot_general(left, right, (((ca,), (cb,)), ((), ())), preferred_element_type=F32)


def iota(shape, dim):
    return lax.broadcasted_iota(jnp.int32, shape, dim)


def inverse(lower, size):
    row, col = iota((size, size), 0), iota((size, size), 1)
    level = row ^ col
    inv = jnp.where(row == col, 1.0, jnp.where((level == 1), -lower, 0.0))
    step = 2
    while step < size:
        part = jnp.where((level >= step) & (level < 2 * step), lower, 0.0)
        inv_pair = split(inv)
        inv = inv - mm(inv_pair, split(mm(split(part), inv_pair)))
        step *= 2
    return inv


def places_root(index):
    places = (index * T + iota((T, 1), 0) + 1).astype(F32)
    return 1.0 / jnp.sqrt(places)


def keys_kernel(raw_ref, k_ref, norm_ref, inv_ref):
    raw = raw_ref[...].astype(F32)
    norm = 1.0 / jnp.sqrt(jnp.sum(raw * raw, axis=1, keepdims=True) + 1e-06)
    key = raw * norm
    k_ref[...] = key
    norm_ref[...] = jnp.broadcast_to(norm, (T, D))
    keys = split(key)
    gram = mm(keys, keys, (1, 1))
    row, col = iota((T, T), 0), iota((T, T), 1)
    lower = jnp.where(row > col, 2.0 * gram, 0.0)
    half = T // 2
    first = inverse(lower[:half, :half], half)
    second = inverse(lower[half:, half:], half)
    corner = -mm(split(second), split(mm(split(lower[half:, :half]), split(first))))
    inv_ref[:half, :half] = first
    inv_ref[:half, half:] = jnp.zeros((half, half), F32)
    inv_ref[half:, :half] = corner
    inv_ref[half:, half:] = second


def load_heads(pairs):
    for source, room in pairs:
        room[...] = source[...].astype(F32)
    return [pl.ds(head, T, stride=2) for head in range(2)]


def causal_scores(query, keys, root):
    row, col = iota((T, T), 0), iota((T, T), 1)
    return jnp.where(row >= col, mm(exact(query.astype(BF16)), keys, (1, 1)), 0.0) * root


def before_kernel(index_ref, k_ref, inv_ref, q_ref, v_ref, d_ref, send_ref, w_ref, x_ref, qs_ref, vs_ref, ds_ref):
    rows = load_heads([(q_ref, qs_ref), (v_ref, vs_ref), (d_ref, ds_ref)])
    root = places_root(index_ref[0])
    key = k_ref[...]
    keys, invs, keys_t = split(key), split(inv_ref[...]), split(key.T)
    w = 2.0 * mm(invs, keys)
    w_ref[...] = w
    ws = split(w)
    eye = jnp.where(iota((D, D), 0) == iota((D, D), 1), 1.0, 0.0)
    send_ref[:, :D] = eye - mm(keys_t, ws)
    value = jnp.concatenate([vs_ref[r, :] for r in rows], axis=1).astype(BF16)
    x0 = mm(invs, exact(value))
    x_ref[...] = x0
    send_ref[:, D : 3 * D] = mm(keys_t, split(x0))
    for head in range(2):
        query = qs_ref[rows[head], :]
        grad = exact(ds_ref[rows[head], :].astype(BF16))
        qhat = query * root - mm(split(causal_scores(query, keys, root)), ws)
        send_ref[:, (3 + head) * D : (4 + head) * D] = mm(split(qhat.T), grad)


def side_kernel(index_ref, sent_ref, k_ref, inv_ref, q_ref, d_ref, m_ref, z_ref, qs_ref, ds_ref):
    del sent_ref
    rows = load_heads([(q_ref, qs_ref), (d_ref, ds_ref)])
    root = places_root(index_ref[0])
    keys, inv_t = split(k_ref[...]), split(inv_ref[...].T)
    m_ref[...] = mm(inv_t, keys)
    back = []
    for head in range(2):
        score = causal_scores(qs_ref[rows[head], :], keys, root)
        back.append(mm(split(score.T), exact(ds_ref[rows[head], :].astype(BF16))))
    z_ref[...] = mm(inv_t, split(jnp.concatenate(back, axis=1)))


def pair_kernel(index_ref, got_ref, send_ref):
    core = index_ref[0] % 2
    at_b = pl.ds(pl.multiple_of(D + core * D, D), D)
    at_g = pl.ds(pl.multiple_of(3 * D + core * D, D), D)
    low, up = got_ref[0, :, :D], got_ref[1, :, :D]
    ahead = mm(split(up), split(jnp.concatenate([low, got_ref[0, :, at_b]], axis=1)))
    send_ref[:, :D] = ahead[:, :D]
    send_ref[:, D : 2 * D] = ahead[:, D:] + got_ref[1, :, at_b]
    send_ref[:, 2 * D :] = got_ref[0, :, at_g] + mm(split(low.T), split(got_ref[1, :, at_g]))


def joined(low, up):
    ahead = mm(split(up[:, :D]), split(low[:, : 2 * D]))
    state = ahead[:, D:] + up[:, D : 2 * D]
    gradient = low[:, 2 * D :] + mm(split(low[:, :D].T), split(up[:, 2 * D :]))
    return jnp.concatenate([ahead[:, :D], state, gradient], axis=1)


def block_kernel(index_ref, got_ref, send_ref, block_ref, halves_ref):
    block = index_ref[0] // 8
    low = joined(got_ref[0], got_ref[1])
    up = joined(got_ref[2], got_ref[3])
    halves_ref[0] = low
    halves_ref[1] = up
    whole = joined(low, up)
    block_ref[...] = whole
    send_ref[...] = jnp.where(block == 3, whole[:, 2 * D :], whole[:, D : 2 * D])


def place_kernel(index_ref, sent_ref, got_ref, halves_ref, track_ref):
    del sent_ref
    chip = (index_ref[0] // 2) % 4
    eye = jnp.where(iota((D, D), 0) == iota((D, D), 1), 1.0, 0.0)
    blank = jnp.concatenate([eye, jnp.zeros((D, D), F32)], axis=1)
    below = halves_ref[0, :, : 2 * D]
    above = jnp.concatenate([halves_ref[1, :, :D].T, halves_ref[1, :, 2 * D :]], axis=1)
    outer = chip == 3
    step = mm(
        split(jnp.where(outer, got_ref[2, :, :D], got_ref[1, :, :D].T)), split(jnp.where(outer, below, above))
    )
    add = jnp.where(outer, got_ref[2, :, D : 2 * D], got_ref[1, :, 2 * D :])
    step = jnp.concatenate([step[:, :D], step[:, D:] + add], axis=1)
    track_ref[0] = jnp.where(
        chip == 0, blank, jnp.where(chip == 1, got_ref[0, :, : 2 * D], jnp.where(chip == 2, below, step))
    )
    last = jnp.concatenate([got_ref[3, :, :D].T, got_ref[3, :, 2 * D :]], axis=1)
    track_ref[1] = jnp.where(chip == 3, blank, jnp.where(chip == 2, last, jnp.where(chip == 1, above, step)))


def hop_kernel(downward, index_ref, got_ref, block_ref, send_ref):
    down = index_ref[0] // 8 == downward
    whole = block_ref[:, :D]
    own = jnp.where(down, block_ref[:, 2 * D :], block_ref[:, D : 2 * D])
    send_ref[...] = own + mm(split(jnp.where(down, whole.T, whole)), split(got_ref[...]))


def top_kernel(index_ref, first_ref, second_ref, third_ref, track_ref, send_ref):
    block = index_ref[0] // 8
    first, second, third = first_ref[...], second_ref[...], third_ref[...]
    state = jnp.where(block == 1, first, jnp.where(block == 2, second, jnp.where(block == 3, third, 0.0)))
    adjoint = jnp.where(block == 2, first, jnp.where(block == 1, second, jnp.where(block == 0, third, 0.0)))
    send_ref[:, :D] = track_ref[0, :, D:] + mm(split(track_ref[0, :, :D]), split(state))
    send_ref[:, D:] = track_ref[1, :, D:] + mm(split(track_ref[1, :, :D]), split(adjoint))


def after_kernel(index_ref, pair_ref, got_ref, q_ref, d_ref, k_ref, w_ref, m_ref, x0_ref, z0_ref,
                 gk_ref, s_ref, x_ref, z_ref, qs_ref, ds_ref):
    qs_ref[...] = q_ref[...].astype(F32)
    ds_ref[...] = d_ref[...].astype(F32)
    rows = [pl.ds(head, T, stride=2) for head in range(2)]
    upper = index_ref[0] % 2 == 1
    state = jnp.concatenate([got_ref[0, :, :D], got_ref[1, :, :D]], axis=1)
    adjoint = jnp.concatenate([got_ref[0, :, D:], got_ref[1, :, D:]], axis=1)
    step = mm(
        split(jnp.where(upper, pair_ref[0, :, :D], pair_ref[1, :, :D].T)),
        split(jnp.where(upper, state, adjoint)),
    )
    state = jnp.where(upper, step + pair_ref[0, :, D : 3 * D], state)
    adjoint = jnp.where(upper, adjoint, step + pair_ref[1, :, 3 * D :])
    s_ref[...] = state
    states, adjoints = split(state), split(adjoint)
    root = places_root(index_ref[0])
    keys = split(k_ref[...])
    row, col = iota((T, T), 0), iota((T, T), 1)
    x = x0_ref[...] - mm(split(w_ref[...]), states)
    x_ref[...] = x
    xs = split(x)
    z = z0_ref[...] + mm(split(m_ref[...]), adjoints)
    z_ref[...] = z
    zs = split(z)
    edge = jnp.where(row > col, mm(zs, xs, (1, 1)), 0.0)
    gk = mm(xs, adjoints, (1, 1)) - 2.0 * mm(zs, states, (1, 1)) - 2.0 * mm(split(edge + edge.T), keys)
    for head in range(2):
        part = slice(head * D, (head + 1) * D)
        query = exact(qs_ref[rows[head], :].astype(BF16))
        grad = exact(ds_ref[rows[head], :].astype(BF16))
        mix = jnp.where(row >= col, mm(grad, tuple(s[:, part] for s in xs), (1, 1)), 0.0) * root
        gk = gk + mm(split(mix.T), query)
    gk_ref[...] = gk


def rest_kernel(index_ref, q_ref, d_ref, k_ref, s_ref, x_ref, z_ref, out_ref, gq_ref, gv_ref, qs_ref, ds_ref,
                os_ref, gs_ref, zs_ref):
    qs_ref[...] = q_ref[...].astype(F32)
    ds_ref[...] = d_ref[...].astype(F32)
    rows = [pl.ds(head, T, stride=2) for head in range(2)]
    root = places_root(index_ref[0])
    keys = split(k_ref[...])
    row, col = iota((T, T), 0), iota((T, T), 1)
    states, xs = split(s_ref[...]), split(x_ref[...])
    for head in range(2):
        part = slice(head * D, (head + 1) * D)
        head_states, head_xs = tuple(s[:, part] for s in states), tuple(s[:, part] for s in xs)
        query = exact(qs_ref[rows[head], :].astype(BF16))
        grad = exact(ds_ref[rows[head], :].astype(BF16))
        score = jnp.where(row >= col, mm(query, keys, (1, 1)), 0.0)
        os_ref[rows[head], :] = root * (mm(query, head_states) + mm(split(score), head_xs))
        mix = jnp.where(row >= col, mm(grad, head_xs, (1, 1)), 0.0)
        gs_ref[rows[head], :] = root * (mm(grad, head_states, (1, 1)) + mm(split(mix), keys))
        zs_ref[rows[head], :] = z_ref[:, part]
    out_ref[...] = os_ref[...].astype(BF16)
    gq_ref[...] = gs_ref[...].astype(BF16)
    gv_ref[...] = zs_ref[...].astype(BF16)


def sum_kernel(got_ref, out_ref):
    out_ref[...] = jnp.broadcast_to(jnp.sum(got_ref[...], axis=0, keepdims=True), out_ref.shape)


def key_kernel(got_ref, k_ref, norm_ref, out_ref):
    total, key = got_ref[...], k_ref[...]
    along = jnp.sum(total * key, axis=1, keepdims=True)
    out_ref[...] = ((total - key * along) * norm_ref[...]).astype(BF16)


def call(kernel, outs, *operands, scratch=(), scalars=1, cost=None):
    spaces = [pltpu.SMEM] * scalars + [pltpu.VMEM] * (len(operands) - scalars)
    single = not isinstance(outs, list)
    shapes = [outs] if single else outs
    result = pl.pallas_call(
        kernel,
        out_shape=[jax.ShapeDtypeStruct(*s) for s in shapes],
        in_specs=[pl.BlockSpec(memory_space=space) for space in spaces],
        out_specs=[pl.BlockSpec(memory_space=pltpu.VMEM)] * len(shapes),
        scratch_shapes=list(scratch),
        compiler_params=pltpu.CompilerParams(vmem_limit_bytes=VMEM_LIMIT),
        cost_estimate=cost,
    )(*operands)
    return result[0] if single else result


def exchange(x, groups):
    return lax.all_gather(x, "seq", axis_index_groups=groups)


def near(*offsets):
    groups, taken = [], set()
    for i in range(PARTS):
        if i not in taken:
            groups.append([i + offset for offset in offsets])
            taken.update(groups[-1])
    return groups


def hop(x, *moves):
    return lax.ppermute(x, "seq", [(8 * a + i, 8 * b + i) for a, b in moves for i in range(8)])


def shards(queries, raw_keys, values, cotangent):
    index = lax.axis_index("seq").astype(jnp.int32).reshape(1)
    q = queries.reshape(2 * T, D)
    v = values.reshape(2 * T, D)
    d = cotangent.reshape(2 * T, D)
    wide = pltpu.VMEM((2 * T, D), F32)
    key, norm, inv = call(
        keys_kernel, [((T, D), F32), ((T, D), F32), ((T, T), F32)], raw_keys, scalars=0, cost=LONG
    )
    send, w, x0 = call(
        before_kernel,
        [((D, 5 * D), F32), ((T, D), F32), ((T, 2 * D), F32)],
        index, key, inv, q, v, d,
        scratch=[wide] * 3,
    )
    pair = exchange(send, near(0, 1))
    send = call(pair_kernel, ((D, 3 * D), F32), index, pair)
    chips = exchange(send, near(0, 2, 4, 6))
    send, block, halves = call(
        block_kernel, [((D, D), F32), ((D, 3 * D), F32), ((2, D, 3 * D), F32)], index, chips
    )
    first = hop(send, (0, 1), (3, 2))
    track = call(place_kernel, ((2, D, 2 * D), F32), index, send, chips, halves, cost=SHORT)
    m, z0 = call(
        side_kernel,
        [((T, D), F32), ((T, 2 * D), F32)],
        index, send, key, inv, q, d,
        scratch=[wide] * 2,
        cost=SHORT,
    )
    send = call(functools.partial(hop_kernel, 2), ((D, D), F32), index, first, block)
    second = hop(send, (1, 2), (2, 1))
    send = call(functools.partial(hop_kernel, 1), ((D, D), F32), index, second, block)
    third = hop(send, (2, 3), (1, 0))
    send = call(top_kernel, ((D, 2 * D), F32), index, first, second, third, track)
    got = exchange(send, near(0, 1))
    gk, state, x, z = call(
        after_kernel,
        [((T, D), F32), ((D, 2 * D), F32), ((T, 2 * D), F32), ((T, 2 * D), F32)],
        index, pair, got, q, d, key, w, m, x0, z0,
        scratch=[wide] * 2,
    )
    peers = lax.axis_size("head")
    pieces = lax.all_to_all(gk.reshape(peers, T // peers, D), "head", 0, 0)
    out, gq, gv = call(
        rest_kernel,
        [((2 * T, D), BF16)] * 3,
        index, q, d, key, state, x, z,
        scratch=[wide] * 5,
        cost=LONG,
    )
    totals = call(sum_kernel, ((peers, T // peers, D), F32), pieces, scalars=0)
    total = lax.all_to_all(totals, "head", 0, 0).reshape(T, D)
    gkey = call(key_kernel, ((T, D), BF16), total, key, norm, scalars=0)
    shape = queries.shape
    return out.reshape(shape), gq.reshape(shape), gkey, gv.reshape(shape)


def solution(mesh):
    split_both = P("seq", "head", None)
    keys_only = P("seq", None)
    return jax.shard_map(
        shards,
        mesh=mesh,
        in_specs=(split_both, keys_only, split_both, split_both),
        out_specs=(split_both, split_both, keys_only, split_both),
        check_vma=False,
    )
```

```python
import jax
import jax.numpy as jnp
from jax import lax
from jax.experimental import pallas as pl
from jax.experimental.pallas import tpu as pltpu
from jax.sharding import PartitionSpec as P

T = 256
PARTS = 32
D = 128
F32 = jnp.float32
BF16 = jnp.bfloat16
VMEM_LIMIT = 48 * 1024 * 1024
SHORT = pl.CostEstimate(flops=500000000, bytes_accessed=1000000, transcendentals=0)
LONG = pl.CostEstimate(flops=4000000000, bytes_accessed=4000000, transcendentals=0)


def split(x):
    high = x.astype(BF16)
    return high, (x - high.astype(F32)).astype(BF16)


def exact(x):
    return x, None


def mm(a, b, over=(1, 0)):
    ca, cb = over
    terms = [(a[0], b[0])]
    if b[1] is not None:
        terms.append((a[0], b[1]))
    if a[1] is not None:
        terms.append((a[1], b[0]))
    left = jnp.concatenate([t[0] for t in terms], axis=ca)
    right = jnp.concatenate([t[1] for t in terms], axis=cb)
    return lax.dot_general(left, right, (((ca,), (cb,)), ((), ())), preferred_element_type=F32)


def iota(shape, dim):
    return lax.broadcasted_iota(jnp.int32, shape, dim)


def inverse(lower, size):
    row, col = iota((size, size), 0), iota((size, size), 1)
    level = row ^ col
    inv = jnp.where(row == col, 1.0, jnp.where((level == 1), -lower, 0.0))
    step = 2
    while step < size:
        part = jnp.where((level >= step) & (level < 2 * step), lower, 0.0)
        inv_pair = split(inv)
        inv = inv - mm(inv_pair, split(mm(split(part), inv_pair)))
        step *= 2
    return inv


def places_root(index):
    places = (index * T + iota((T, 1), 0) + 1).astype(F32)
    return 1.0 / jnp.sqrt(places)


def keys_kernel(raw_ref, k_ref, norm_ref, inv_ref):
    raw = raw_ref[...].astype(F32)
    norm = 1.0 / jnp.sqrt(jnp.sum(raw * raw, axis=1, keepdims=True) + 1e-06)
    key = raw * norm
    k_ref[...] = key
    norm_ref[...] = jnp.broadcast_to(norm, (T, D))
    keys = split(key)
    gram = mm(keys, keys, (1, 1))
    row, col = iota((T, T), 0), iota((T, T), 1)
    lower = jnp.where(row > col, 2.0 * gram, 0.0)
    half = T // 2
    first = inverse(lower[:half, :half], half)
    second = inverse(lower[half:, half:], half)
    corner = -mm(split(second), split(mm(split(lower[half:, :half]), split(first))))
    inv_ref[:half, :half] = first
    inv_ref[:half, half:] = jnp.zeros((half, half), F32)
    inv_ref[half:, :half] = corner
    inv_ref[half:, half:] = second


def load_heads(pairs):
    for source, room in pairs:
        room[...] = source[...].astype(F32)
    return [pl.ds(head, T, stride=2) for head in range(2)]


def causal_scores(query, keys, root):
    row, col = iota((T, T), 0), iota((T, T), 1)
    return jnp.where(row >= col, mm(exact(query.astype(BF16)), keys, (1, 1)), 0.0) * root


def before_kernel(index_ref, k_ref, inv_ref, q_ref, v_ref, d_ref, send_ref, w_ref, x_ref, qs_ref, vs_ref, ds_ref):
    rows = load_heads([(q_ref, qs_ref), (v_ref, vs_ref), (d_ref, ds_ref)])
    root = places_root(index_ref[0])
    key = k_ref[...]
    keys, invs, keys_t = split(key), split(inv_ref[...]), split(key.T)
    w = 2.0 * mm(invs, keys)
    w_ref[...] = w
    ws = split(w)
    eye = jnp.where(iota((D, D), 0) == iota((D, D), 1), 1.0, 0.0)
    send_ref[:, :D] = eye - mm(keys_t, ws)
    value = jnp.concatenate([vs_ref[r, :] for r in rows], axis=1).astype(BF16)
    x0 = mm(invs, exact(value))
    x_ref[...] = x0
    send_ref[:, D : 3 * D] = mm(keys_t, split(x0))
    for head in range(2):
        query = qs_ref[rows[head], :]
        grad = exact(ds_ref[rows[head], :].astype(BF16))
        qhat = query * root - mm(split(causal_scores(query, keys, root)), ws)
        send_ref[:, (3 + head) * D : (4 + head) * D] = mm(split(qhat.T), grad)


def side_kernel(index_ref, sent_ref, k_ref, inv_ref, q_ref, d_ref, m_ref, z_ref, qs_ref, ds_ref):
    del sent_ref
    rows = load_heads([(q_ref, qs_ref), (d_ref, ds_ref)])
    root = places_root(index_ref[0])
    keys, inv_t = split(k_ref[...]), split(inv_ref[...].T)
    m_ref[...] = mm(inv_t, keys)
    back = []
    for head in range(2):
        score = causal_scores(qs_ref[rows[head], :], keys, root)
        back.append(mm(split(score.T), exact(ds_ref[rows[head], :].astype(BF16))))
    z_ref[...] = mm(inv_t, split(jnp.concatenate(back, axis=1)))


def then(first, second):
    step = mm(split(second[:, :D]), split(first))
    return jnp.concatenate([step[:, :D], step[:, D:] + second[:, D:]], axis=1)


def along(index_ref, size, unit):
    place = (index_ref[0] // unit) % size
    return jnp.where(index_ref[0] % 2 == 1, size - 1 - place, place)


def pair_kernel(index_ref, got_ref, send_ref):
    down = index_ref[0] % 2 == 1

    def ranges(i):
        return jnp.concatenate(
            [
                jnp.where(down, got_ref[1 - i, :, :D].T, got_ref[i, :, :D]),
                jnp.where(down, got_ref[1 - i, :, 3 * D :], got_ref[i, :, D : 3 * D]),
            ],
            axis=1,
        )

    send_ref[...] = then(ranges(0), ranges(1))


def chip_kernel(index_ref, got_ref, send_ref):
    down, right = index_ref[0] % 2 == 1, (index_ref[0] // 2) % 2 == 1
    first, second = [halved(jnp.where(down, got_ref[1 - i], got_ref[i]), right) for i in range(2)]
    send_ref[...] = then(first, second)


def halved(x, right):
    return jnp.concatenate([x[:, :D], jnp.where(right, x[:, 2 * D :], x[:, D : 2 * D])], axis=1)


def block_kernel(index_ref, got_ref, send_ref, block_ref):
    down = index_ref[0] % 2 == 1
    first, second = [jnp.where(down, got_ref[1 - i], got_ref[i]) for i in range(2)]
    whole = then(first, second)
    block_ref[...] = whole
    send_ref[...] = whole[:, D:]


def hop_kernel(got_ref, block_ref, send_ref):
    send_ref[...] = block_ref[:, D:] + mm(split(block_ref[:, :D]), split(got_ref[...]))


def top_kernel(index_ref, first_ref, second_ref, third_ref, units_ref, chips_ref, send_ref):
    down, right = index_ref[0] % 2 == 1, (index_ref[0] // 2) % 2 == 1
    place = along(index_ref, 4, 8)
    got = jnp.where(
        place == 1, first_ref[...], jnp.where(place == 2, second_ref[...], jnp.where(place == 3, third_ref[...], 0.0))
    )
    unit = jnp.where(down, units_ref[1], units_ref[0])
    later = unit[:, D:] + mm(split(unit[:, :D]), split(got))
    got = jnp.where(along(index_ref, 2, 4) == 1, later, got)
    send_ref[:, :D] = got
    chip = halved(jnp.where(down, chips_ref[1], chips_ref[0]), right)
    send_ref[:, D:] = chip[:, D:] + mm(split(chip[:, :D]), split(got))


def after_kernel(index_ref, pair_ref, got_ref, q_ref, d_ref, k_ref, w_ref, m_ref, x0_ref, z0_ref,
                 gk_ref, s_ref, x_ref, z_ref, qs_ref, ds_ref):
    qs_ref[...] = q_ref[...].astype(F32)
    ds_ref[...] = d_ref[...].astype(F32)
    rows = [pl.ds(head, T, stride=2) for head in range(2)]
    upper = index_ref[0] % 2 == 1
    right = (index_ref[0] // 2) % 2 == 1
    state, adjoint = [
        jnp.concatenate(
            [jnp.where(right == flip, got_ref[i, :, :D], got_ref[i, :, D:]) for i in (core, core + 2)], axis=1
        )
        for core, flip in ((0, False), (1, True))
    ]
    step = mm(
        split(jnp.where(upper, pair_ref[0, :, :D], pair_ref[1, :, :D].T)),
        split(jnp.where(upper, state, adjoint)),
    )
    state = jnp.where(upper, step + pair_ref[0, :, D : 3 * D], state)
    adjoint = jnp.where(upper, adjoint, step + pair_ref[1, :, 3 * D :])
    s_ref[...] = state
    states, adjoints = split(state), split(adjoint)
    root = places_root(index_ref[0])
    keys = split(k_ref[...])
    row, col = iota((T, T), 0), iota((T, T), 1)
    x = x0_ref[...] - mm(split(w_ref[...]), states)
    x_ref[...] = x
    xs = split(x)
    z = z0_ref[...] + mm(split(m_ref[...]), adjoints)
    z_ref[...] = z
    zs = split(z)
    edge = jnp.where(row > col, mm(zs, xs, (1, 1)), 0.0)
    gk = mm(xs, adjoints, (1, 1)) - 2.0 * mm(zs, states, (1, 1)) - 2.0 * mm(split(edge + edge.T), keys)
    for head in range(2):
        part = slice(head * D, (head + 1) * D)
        query = exact(qs_ref[rows[head], :].astype(BF16))
        grad = exact(ds_ref[rows[head], :].astype(BF16))
        mix = jnp.where(row >= col, mm(grad, tuple(s[:, part] for s in xs), (1, 1)), 0.0) * root
        gk = gk + mm(split(mix.T), query)
    gk_ref[...] = gk


def rest_kernel(index_ref, q_ref, d_ref, k_ref, s_ref, x_ref, z_ref, out_ref, gq_ref, gv_ref, qs_ref, ds_ref,
                os_ref, gs_ref, zs_ref):
    qs_ref[...] = q_ref[...].astype(F32)
    ds_ref[...] = d_ref[...].astype(F32)
    rows = [pl.ds(head, T, stride=2) for head in range(2)]
    root = places_root(index_ref[0])
    keys = split(k_ref[...])
    row, col = iota((T, T), 0), iota((T, T), 1)
    states, xs = split(s_ref[...]), split(x_ref[...])
    for head in range(2):
        part = slice(head * D, (head + 1) * D)
        head_states, head_xs = tuple(s[:, part] for s in states), tuple(s[:, part] for s in xs)
        query = exact(qs_ref[rows[head], :].astype(BF16))
        grad = exact(ds_ref[rows[head], :].astype(BF16))
        score = jnp.where(row >= col, mm(query, keys, (1, 1)), 0.0)
        os_ref[rows[head], :] = root * (mm(query, head_states) + mm(split(score), head_xs))
        mix = jnp.where(row >= col, mm(grad, head_xs, (1, 1)), 0.0)
        gs_ref[rows[head], :] = root * (mm(grad, head_states, (1, 1)) + mm(split(mix), keys))
        zs_ref[rows[head], :] = z_ref[:, part]
    out_ref[...] = os_ref[...].astype(BF16)
    gq_ref[...] = gs_ref[...].astype(BF16)
    gv_ref[...] = zs_ref[...].astype(BF16)


def sum_kernel(got_ref, out_ref):
    out_ref[...] = jnp.broadcast_to(jnp.sum(got_ref[...], axis=0, keepdims=True), out_ref.shape)


def key_kernel(got_ref, k_ref, norm_ref, out_ref):
    total, key = got_ref[...], k_ref[...]
    along = jnp.sum(total * key, axis=1, keepdims=True)
    out_ref[...] = ((total - key * along) * norm_ref[...]).astype(BF16)


def call(kernel, outs, *operands, scratch=(), scalars=1, cost=None):
    spaces = [pltpu.SMEM] * scalars + [pltpu.VMEM] * (len(operands) - scalars)
    single = not isinstance(outs, list)
    shapes = [outs] if single else outs
    result = pl.pallas_call(
        kernel,
        out_shape=[jax.ShapeDtypeStruct(*s) for s in shapes],
        in_specs=[pl.BlockSpec(memory_space=space) for space in spaces],
        out_specs=[pl.BlockSpec(memory_space=pltpu.VMEM)] * len(shapes),
        scratch_shapes=list(scratch),
        compiler_params=pltpu.CompilerParams(vmem_limit_bytes=VMEM_LIMIT),
        cost_estimate=cost,
    )(*operands)
    return result[0] if single else result


def exchange(x, groups):
    return lax.all_gather(x, "seq", axis_index_groups=groups)


def near(*offsets):
    groups, taken = [], set()
    for i in range(PARTS):
        if i not in taken:
            groups.append([i + offset for offset in offsets])
            taken.update(groups[-1])
    return groups


def hop(x, place):
    up = [(8 * place + i, 8 * place + i + 8) for i in range(0, 8, 2)]
    return lax.ppermute(x, "seq", up + [(PARTS - 1 - a, PARTS - 1 - b) for a, b in up])


def shards(queries, raw_keys, values, cotangent):
    index = lax.axis_index("seq").astype(jnp.int32).reshape(1)
    q = queries.reshape(2 * T, D)
    v = values.reshape(2 * T, D)
    d = cotangent.reshape(2 * T, D)
    wide = pltpu.VMEM((2 * T, D), F32)
    key, norm, inv = call(
        keys_kernel, [((T, D), F32), ((T, D), F32), ((T, T), F32)], raw_keys, scalars=0, cost=LONG
    )
    send, w, x0 = call(
        before_kernel,
        [((D, 5 * D), F32), ((T, D), F32), ((T, 2 * D), F32)],
        index, key, inv, q, v, d,
        scratch=[wide] * 3,
    )
    pair = exchange(send, near(0, 1))
    send = call(pair_kernel, ((D, 3 * D), F32), index, pair)
    chips = exchange(send, near(0, 2))
    send = call(chip_kernel, ((D, 2 * D), F32), index, chips)
    units = exchange(send, near(0, 4))
    send, block = call(block_kernel, [((D, D), F32), ((D, 2 * D), F32)], index, units)
    first = hop(send, 0)
    m, z0 = call(
        side_kernel,
        [((T, D), F32), ((T, 2 * D), F32)],
        index, send, key, inv, q, d,
        scratch=[wide] * 2,
        cost=SHORT,
    )
    send = call(hop_kernel, ((D, D), F32), first, block, scalars=0)
    second = hop(send, 1)
    send = call(hop_kernel, ((D, D), F32), second, block, scalars=0)
    third = hop(send, 2)
    send = call(top_kernel, ((D, 2 * D), F32), index, first, second, third, units, chips)
    got = exchange(send, near(0, 1, 2, 3))
    gk, state, x, z = call(
        after_kernel,
        [((T, D), F32), ((D, 2 * D), F32), ((T, 2 * D), F32), ((T, 2 * D), F32)],
        index, pair, got, q, d, key, w, m, x0, z0,
        scratch=[wide] * 2,
    )
    peers = lax.axis_size("head")
    pieces = lax.all_to_all(gk.reshape(peers, T // peers, D), "head", 0, 0)
    out, gq, gv = call(
        rest_kernel,
        [((2 * T, D), BF16)] * 3,
        index, q, d, key, state, x, z,
        scratch=[wide] * 5,
        cost=LONG,
    )
    totals = call(sum_kernel, ((peers, T // peers, D), F32), pieces, scalars=0)
    total = lax.all_to_all(totals, "head", 0, 0).reshape(T, D)
    gkey = call(key_kernel, ((T, D), BF16), total, key, norm, scalars=0)
    shape = queries.shape
    return out.reshape(shape), gq.reshape(shape), gkey, gv.reshape(shape)


def solution(mesh):
    split_both = P("seq", "head", None)
    keys_only = P("seq", None)
    return jax.shard_map(
        shards,
        mesh=mesh,
        in_specs=(split_both, keys_only, split_both, split_both),
        out_specs=(split_both, split_both, keys_only, split_both),
        check_vma=False,
    )
```

```python
import jax
import jax.numpy as jnp
from jax import lax
from jax.experimental import pallas as pl
from jax.experimental.pallas import tpu as pltpu
from jax.sharding import PartitionSpec as P

T = 256
PARTS = 32
D = 128
F32 = jnp.float32
BF16 = jnp.bfloat16
VMEM_LIMIT = 48 * 1024 * 1024
SHORT = pl.CostEstimate(flops=500000000, bytes_accessed=1000000, transcendentals=0)
LONG = pl.CostEstimate(flops=4000000000, bytes_accessed=4000000, transcendentals=0)


def split(x):
    high = x.astype(BF16)
    return high, (x - high.astype(F32)).astype(BF16)


def exact(x):
    return x, None


def mm(a, b, over=(1, 0)):
    ca, cb = over
    terms = [(a[0], b[0])]
    if b[1] is not None:
        terms.append((a[0], b[1]))
    if a[1] is not None:
        terms.append((a[1], b[0]))
    left = jnp.concatenate([t[0] for t in terms], axis=ca)
    right = jnp.concatenate([t[1] for t in terms], axis=cb)
    return lax.dot_general(left, right, (((ca,), (cb,)), ((), ())), preferred_element_type=F32)


def iota(shape, dim):
    return lax.broadcasted_iota(jnp.int32, shape, dim)


def inverses(lowers, size):
    row, col = iota((size, size), 0), iota((size, size), 1)
    level = row ^ col

    def part(low, high):
        return [jnp.where((level >= low) & (level < high), lower, 0.0) for lower in lowers]

    edges = part(1, 4)
    starts = [jnp.where(row == col, 1.0, -edge) for edge in edges]
    edges = [split(edge) for edge in edges]
    squares = [split(mm(edge, edge)) for edge in edges]
    invs = [start + mm(square, split(start)) for start, square in zip(starts, squares)]
    step = 4
    while step < size:
        pairs = [split(inv) for inv in invs]
        if 4 * step <= size:
            edges = [split(mm(pair, split(edge))) for pair, edge in zip(pairs, part(step, 4 * step))]
            starts = [mm(edge, pair) for edge, pair in zip(edges, pairs)]
            squares = [mm(edge, edge) for edge in edges]
            starts = [inv - start for inv, start in zip(invs, starts)]
            invs = [start + mm(split(square), split(start)) for start, square in zip(starts, squares)]
            step *= 4
        else:
            edges = [split(mm(split(edge), pair)) for pair, edge in zip(pairs, part(step, 2 * step))]
            invs = [inv - mm(pair, edge) for inv, pair, edge in zip(invs, pairs, edges)]
            step *= 2
    return invs


def places_root(index):
    places = (index * T + iota((T, 1), 0) + 1).astype(F32)
    return 1.0 / jnp.sqrt(places)


def keys_kernel(raw_ref, k_ref, norm_ref, inv_ref):
    raw = raw_ref[...].astype(F32)
    norm = 1.0 / jnp.sqrt(jnp.sum(raw * raw, axis=1, keepdims=True) + 1e-06)
    key = raw * norm
    k_ref[...] = key
    norm_ref[...] = jnp.broadcast_to(norm, (T, D))
    keys = split(key)
    gram = mm(keys, keys, (1, 1))
    row, col = iota((T, T), 0), iota((T, T), 1)
    lower = jnp.where(row > col, 2.0 * gram, 0.0)
    half = T // 2
    first, second = inverses([lower[:half, :half], lower[half:, half:]], half)
    corner = -mm(split(second), split(mm(split(lower[half:, :half]), split(first))))
    inv_ref[:half, :half] = first
    inv_ref[:half, half:] = jnp.zeros((half, half), F32)
    inv_ref[half:, :half] = corner
    inv_ref[half:, half:] = second


def load_heads(pairs):
    for source, room in pairs:
        room[...] = source[...].astype(F32)
    return [pl.ds(head, T, stride=2) for head in range(2)]


def causal_scores(query, keys, root):
    row, col = iota((T, T), 0), iota((T, T), 1)
    return jnp.where(row >= col, mm(exact(query.astype(BF16)), keys, (1, 1)), 0.0) * root


def before_kernel(index_ref, k_ref, inv_ref, q_ref, v_ref, d_ref, send_ref, w_ref, x_ref, qs_ref, vs_ref, ds_ref):
    rows = load_heads([(q_ref, qs_ref), (v_ref, vs_ref), (d_ref, ds_ref)])
    root = places_root(index_ref[0])
    key = k_ref[...]
    keys, invs, keys_t = split(key), split(inv_ref[...]), split(key.T)
    queries = [qs_ref[r, :] for r in rows]
    scores = [causal_scores(query, keys, root) for query in queries]
    w = 2.0 * mm(invs, keys)
    x0 = mm(invs, exact(jnp.concatenate([vs_ref[r, :] for r in rows], axis=1).astype(BF16)))
    w_ref[...] = w
    x_ref[...] = x0
    ws, x0s = split(w), split(x0)
    mixed = [mm(split(score), ws) for score in scores]
    eye = jnp.where(iota((D, D), 0) == iota((D, D), 1), 1.0, 0.0)
    send_ref[:, :D] = eye - mm(keys_t, ws)
    send_ref[:, D : 3 * D] = mm(keys_t, x0s)
    qhats = [split((query * root - mix).T) for query, mix in zip(queries, mixed)]
    grads = [exact(ds_ref[r, :].astype(BF16)) for r in rows]
    back = [mm(qhat, grad) for qhat, grad in zip(qhats, grads)]
    send_ref[:, 3 * D :] = jnp.concatenate(back, axis=1)


def side_kernel(index_ref, sent_ref, k_ref, inv_ref, q_ref, d_ref, m_ref, z_ref, qs_ref, ds_ref):
    del sent_ref
    rows = load_heads([(q_ref, qs_ref), (d_ref, ds_ref)])
    root = places_root(index_ref[0])
    keys, inv_t = split(k_ref[...]), split(inv_ref[...].T)
    m_ref[...] = mm(inv_t, keys)
    back = []
    for head in range(2):
        score = causal_scores(qs_ref[rows[head], :], keys, root)
        back.append(mm(split(score.T), exact(ds_ref[rows[head], :].astype(BF16))))
    z_ref[...] = mm(inv_t, split(jnp.concatenate(back, axis=1)))


def then(first, second):
    step = mm(split(second[:, :D]), split(first))
    return jnp.concatenate([step[:, :D], step[:, D:] + second[:, D:]], axis=1)


def along(index_ref, size, unit):
    place = (index_ref[0] // unit) % size
    return jnp.where(index_ref[0] % 2 == 1, size - 1 - place, place)


def pair_kernel(index_ref, got_ref, send_ref):
    down = index_ref[0] % 2 == 1

    def ranges(i):
        return jnp.concatenate(
            [
                jnp.where(down, got_ref[1 - i, :, :D].T, got_ref[i, :, :D]),
                jnp.where(down, got_ref[1 - i, :, 3 * D :], got_ref[i, :, D : 3 * D]),
            ],
            axis=1,
        )

    send_ref[...] = then(ranges(0), ranges(1))


def chip_kernel(index_ref, got_ref, send_ref):
    down, right = index_ref[0] % 2 == 1, (index_ref[0] // 2) % 2 == 1
    first, second = [halved(jnp.where(down, got_ref[1 - i], got_ref[i]), right) for i in range(2)]
    send_ref[...] = then(first, second)


def halved(x, right):
    return jnp.concatenate([x[:, :D], jnp.where(right, x[:, 2 * D :], x[:, D : 2 * D])], axis=1)


def block_kernel(index_ref, got_ref, send_ref, block_ref):
    down = index_ref[0] % 2 == 1
    first, second = [jnp.where(down, got_ref[1 - i], got_ref[i]) for i in range(2)]
    whole = then(first, second)
    block_ref[...] = whole
    send_ref[...] = whole[:, D:]


def hop_kernel(got_ref, block_ref, send_ref):
    send_ref[...] = block_ref[:, D:] + mm(split(block_ref[:, :D]), split(got_ref[...]))


def top_kernel(index_ref, first_ref, second_ref, third_ref, units_ref, chips_ref, send_ref):
    down, right = index_ref[0] % 2 == 1, (index_ref[0] // 2) % 2 == 1
    place = along(index_ref, 4, 8)
    got = jnp.where(
        place == 1, first_ref[...], jnp.where(place == 2, second_ref[...], jnp.where(place == 3, third_ref[...], 0.0))
    )
    unit = jnp.where(down, units_ref[1], units_ref[0])
    later = unit[:, D:] + mm(split(unit[:, :D]), split(got))
    got = jnp.where(along(index_ref, 2, 4) == 1, later, got)
    send_ref[:, :D] = got
    chip = halved(jnp.where(down, chips_ref[1], chips_ref[0]), right)
    send_ref[:, D:] = chip[:, D:] + mm(split(chip[:, :D]), split(got))


def after_kernel(index_ref, pair_ref, got_ref, q_ref, d_ref, k_ref, w_ref, m_ref, x0_ref, z0_ref,
                 gk_ref, s_ref, x_ref, z_ref, qs_ref, ds_ref):
    qs_ref[...] = q_ref[...].astype(F32)
    ds_ref[...] = d_ref[...].astype(F32)
    rows = [pl.ds(head, T, stride=2) for head in range(2)]
    upper = index_ref[0] % 2 == 1
    right = (index_ref[0] // 2) % 2 == 1
    state, adjoint = [
        jnp.concatenate(
            [jnp.where(right == flip, got_ref[i, :, :D], got_ref[i, :, D:]) for i in (core, core + 2)], axis=1
        )
        for core, flip in ((0, False), (1, True))
    ]
    step = mm(
        split(jnp.where(upper, pair_ref[0, :, :D], pair_ref[1, :, :D].T)),
        split(jnp.where(upper, state, adjoint)),
    )
    state = jnp.where(upper, step + pair_ref[0, :, D : 3 * D], state)
    adjoint = jnp.where(upper, adjoint, step + pair_ref[1, :, 3 * D :])
    s_ref[...] = state
    states, adjoints = split(state), split(adjoint)
    root = places_root(index_ref[0])
    keys = split(k_ref[...])
    row, col = iota((T, T), 0), iota((T, T), 1)
    x = x0_ref[...] - mm(split(w_ref[...]), states)
    x_ref[...] = x
    xs = split(x)
    z = z0_ref[...] + mm(split(m_ref[...]), adjoints)
    z_ref[...] = z
    zs = split(z)
    parts = [slice(head * D, (head + 1) * D) for head in range(2)]
    queries = [exact(qs_ref[r, :].astype(BF16)) for r in rows]
    grads = [exact(ds_ref[r, :].astype(BF16)) for r in rows]
    edge = mm(zs, xs, (1, 1))
    mixed = [mm(grad, tuple(s[:, part] for s in xs), (1, 1)) for grad, part in zip(grads, parts)]
    gk = mm(xs, adjoints, (1, 1)) - 2.0 * mm(zs, states, (1, 1))
    edge = jnp.where(row > col, edge, 0.0)
    mixed = [split((jnp.where(row >= col, mix, 0.0) * root).T) for mix in mixed]
    last = [mm(mix, query) for mix, query in zip(mixed, queries)]
    gk = gk - 2.0 * mm(split(edge + edge.T), keys) + last[0] + last[1]
    gk_ref[...] = gk


def rest_kernel(index_ref, q_ref, d_ref, k_ref, s_ref, x_ref, z_ref, out_ref, gq_ref, gv_ref, qs_ref, ds_ref,
                os_ref, gs_ref, zs_ref):
    qs_ref[...] = q_ref[...].astype(F32)
    ds_ref[...] = d_ref[...].astype(F32)
    rows = [pl.ds(head, T, stride=2) for head in range(2)]
    root = places_root(index_ref[0])
    keys = split(k_ref[...])
    row, col = iota((T, T), 0), iota((T, T), 1)
    states, xs = split(s_ref[...]), split(x_ref[...])
    for head in range(2):
        part = slice(head * D, (head + 1) * D)
        head_states, head_xs = tuple(s[:, part] for s in states), tuple(s[:, part] for s in xs)
        query = exact(qs_ref[rows[head], :].astype(BF16))
        grad = exact(ds_ref[rows[head], :].astype(BF16))
        score = jnp.where(row >= col, mm(query, keys, (1, 1)), 0.0)
        os_ref[rows[head], :] = root * (mm(query, head_states) + mm(split(score), head_xs))
        mix = jnp.where(row >= col, mm(grad, head_xs, (1, 1)), 0.0)
        gs_ref[rows[head], :] = root * (mm(grad, head_states, (1, 1)) + mm(split(mix), keys))
        zs_ref[rows[head], :] = z_ref[:, part]
    out_ref[...] = os_ref[...].astype(BF16)
    gq_ref[...] = gs_ref[...].astype(BF16)
    gv_ref[...] = zs_ref[...].astype(BF16)


def sum_kernel(got_ref, out_ref):
    out_ref[...] = jnp.broadcast_to(jnp.sum(got_ref[...], axis=0, keepdims=True), out_ref.shape)


def key_kernel(got_ref, k_ref, norm_ref, out_ref):
    total, key = got_ref[...], k_ref[...]
    along = jnp.sum(total * key, axis=1, keepdims=True)
    out_ref[...] = ((total - key * along) * norm_ref[...]).astype(BF16)


def call(kernel, outs, *operands, scratch=(), scalars=1, cost=None):
    spaces = [pltpu.SMEM] * scalars + [pltpu.VMEM] * (len(operands) - scalars)
    single = not isinstance(outs, list)
    shapes = [outs] if single else outs
    result = pl.pallas_call(
        kernel,
        out_shape=[jax.ShapeDtypeStruct(*s) for s in shapes],
        in_specs=[pl.BlockSpec(memory_space=space) for space in spaces],
        out_specs=[pl.BlockSpec(memory_space=pltpu.VMEM)] * len(shapes),
        scratch_shapes=list(scratch),
        compiler_params=pltpu.CompilerParams(vmem_limit_bytes=VMEM_LIMIT),
        cost_estimate=cost,
    )(*operands)
    return result[0] if single else result


def exchange(x, groups):
    return lax.all_gather(x, "seq", axis_index_groups=groups)


def near(*offsets):
    groups, taken = [], set()
    for i in range(PARTS):
        if i not in taken:
            groups.append([i + offset for offset in offsets])
            taken.update(groups[-1])
    return groups


def hop(x, place):
    up = [(8 * place + i, 8 * place + i + 8) for i in range(0, 8, 2)]
    return lax.ppermute(x, "seq", up + [(PARTS - 1 - a, PARTS - 1 - b) for a, b in up])


def shards(queries, raw_keys, values, cotangent):
    index = lax.axis_index("seq").astype(jnp.int32).reshape(1)
    q = queries.reshape(2 * T, D)
    v = values.reshape(2 * T, D)
    d = cotangent.reshape(2 * T, D)
    wide = pltpu.VMEM((2 * T, D), F32)
    key, norm, inv = call(
        keys_kernel, [((T, D), F32), ((T, D), F32), ((T, T), F32)], raw_keys, scalars=0, cost=LONG
    )
    send, w, x0 = call(
        before_kernel,
        [((D, 5 * D), F32), ((T, D), F32), ((T, 2 * D), F32)],
        index, key, inv, q, v, d,
        scratch=[wide] * 3,
    )
    pair = exchange(send, near(0, 1))
    send = call(pair_kernel, ((D, 3 * D), F32), index, pair)
    chips = exchange(send, near(0, 2))
    send = call(chip_kernel, ((D, 2 * D), F32), index, chips)
    units = exchange(send, near(0, 4))
    send, block = call(block_kernel, [((D, D), F32), ((D, 2 * D), F32)], index, units)
    first = hop(send, 0)
    m, z0 = call(
        side_kernel,
        [((T, D), F32), ((T, 2 * D), F32)],
        index, send, key, inv, q, d,
        scratch=[wide] * 2,
        cost=SHORT,
    )
    send = call(hop_kernel, ((D, D), F32), first, block, scalars=0)
    second = hop(send, 1)
    send = call(hop_kernel, ((D, D), F32), second, block, scalars=0)
    third = hop(send, 2)
    send = call(top_kernel, ((D, 2 * D), F32), index, first, second, third, units, chips)
    got = exchange(send, near(0, 1, 2, 3))
    gk, state, x, z = call(
        after_kernel,
        [((T, D), F32), ((D, 2 * D), F32), ((T, 2 * D), F32), ((T, 2 * D), F32)],
        index, pair, got, q, d, key, w, m, x0, z0,
        scratch=[wide] * 2,
    )
    peers = lax.axis_size("head")
    pieces = lax.all_to_all(gk.reshape(peers, T // peers, D), "head", 0, 0)
    out, gq, gv = call(
        rest_kernel,
        [((2 * T, D), BF16)] * 3,
        index, q, d, key, state, x, z,
        scratch=[wide] * 5,
        cost=LONG,
    )
    totals = call(sum_kernel, ((peers, T // peers, D), F32), pieces, scalars=0)
    total = lax.all_to_all(totals, "head", 0, 0).reshape(T, D)
    gkey = call(key_kernel, ((T, D), BF16), total, key, norm, scalars=0)
    shape = queries.shape
    return out.reshape(shape), gq.reshape(shape), gkey, gv.reshape(shape)


def solution(mesh):
    split_both = P("seq", "head", None)
    keys_only = P("seq", None)
    return jax.shard_map(
        shards,
        mesh=mesh,
        in_specs=(split_both, keys_only, split_both, split_both),
        out_specs=(split_both, split_both, keys_only, split_both),
        check_vma=False,
    )
```

```python
import jax
import jax.numpy as jnp
from jax import lax
from jax.experimental import pallas as pl
from jax.experimental.pallas import tpu as pltpu
from jax.sharding import PartitionSpec as P

T = 256
PARTS = 32
D = 128
F32 = jnp.float32
BF16 = jnp.bfloat16
VMEM_LIMIT = 48 * 1024 * 1024
SHORT = pl.CostEstimate(flops=500000000, bytes_accessed=1000000, transcendentals=0)
LONG = pl.CostEstimate(flops=4000000000, bytes_accessed=4000000, transcendentals=0)


def split(x):
    high = x.astype(BF16)
    return high, (x - high.astype(F32)).astype(BF16)


def exact(x):
    return x, None


def mm(a, b, over=(1, 0)):
    ca, cb = over
    terms = [(a[0], b[0])]
    if b[1] is not None:
        terms.append((a[0], b[1]))
    if a[1] is not None:
        terms.append((a[1], b[0]))
    left = jnp.concatenate([t[0] for t in terms], axis=ca)
    right = jnp.concatenate([t[1] for t in terms], axis=cb)
    return lax.dot_general(left, right, (((ca,), (cb,)), ((), ())), preferred_element_type=F32)


def iota(shape, dim):
    return lax.broadcasted_iota(jnp.int32, shape, dim)


def inverses(lowers, size):
    row, col = iota((size, size), 0), iota((size, size), 1)
    level = row ^ col

    def part(low, high):
        return [jnp.where((level >= low) & (level < high), lower, 0.0) for lower in lowers]

    edges = part(1, 4)
    starts = [jnp.where(row == col, 1.0, -edge) for edge in edges]
    edges = [split(edge) for edge in edges]
    squares = [split(mm(edge, edge)) for edge in edges]
    invs = [start + mm(square, split(start)) for start, square in zip(starts, squares)]
    step = 4
    while step < size:
        pairs = [split(inv) for inv in invs]
        if 4 * step <= size:
            edges = [split(mm(pair, split(edge))) for pair, edge in zip(pairs, part(step, 4 * step))]
            starts = [mm(edge, pair) for edge, pair in zip(edges, pairs)]
            squares = [mm(edge, edge) for edge in edges]
            starts = [inv - start for inv, start in zip(invs, starts)]
            invs = [start + mm(split(square), split(start)) for start, square in zip(starts, squares)]
            step *= 4
        else:
            edges = [split(mm(split(edge), pair)) for pair, edge in zip(pairs, part(step, 2 * step))]
            invs = [inv - mm(pair, edge) for inv, pair, edge in zip(invs, pairs, edges)]
            step *= 2
    return invs


def places_root(index):
    places = (index * T + iota((T, 1), 0) + 1).astype(F32)
    return 1.0 / jnp.sqrt(places)


def keys_kernel(raw_ref, k_ref, norm_ref, inv_ref):
    raw = raw_ref[...].astype(F32)
    norm = 1.0 / jnp.sqrt(jnp.sum(raw * raw, axis=1, keepdims=True) + 1e-06)
    key = raw * norm
    k_ref[...] = key
    norm_ref[...] = jnp.broadcast_to(norm, (T, D))
    keys = split(key)
    gram = mm(keys, keys, (1, 1))
    row, col = iota((T, T), 0), iota((T, T), 1)
    lower = jnp.where(row > col, 2.0 * gram, 0.0)
    half = T // 2
    first, second = inverses([lower[:half, :half], lower[half:, half:]], half)
    corner = -mm(split(second), split(mm(split(lower[half:, :half]), split(first))))
    inv_ref[:half, :half] = first
    inv_ref[:half, half:] = jnp.zeros((half, half), F32)
    inv_ref[half:, :half] = corner
    inv_ref[half:, half:] = second


def load_heads(pairs):
    for source, room in pairs:
        room[...] = source[...].astype(F32)
    return [pl.ds(head, T, stride=2) for head in range(2)]


def causal_scores(query, keys, root):
    row, col = iota((T, T), 0), iota((T, T), 1)
    return jnp.where(row >= col, mm(exact(query.astype(BF16)), keys, (1, 1)), 0.0) * root


def before_kernel(index_ref, k_ref, inv_ref, q_ref, v_ref, d_ref, send_ref, w_ref, x_ref, qs_ref, vs_ref, ds_ref):
    rows = load_heads([(q_ref, qs_ref), (v_ref, vs_ref), (d_ref, ds_ref)])
    root = places_root(index_ref[0])
    key = k_ref[...]
    keys, invs, keys_t = split(key), split(inv_ref[...]), split(key.T)
    queries = [qs_ref[r, :] for r in rows]
    scores = [causal_scores(query, keys, root) for query in queries]
    w = 2.0 * mm(invs, keys)
    x0 = mm(invs, exact(jnp.concatenate([vs_ref[r, :] for r in rows], axis=1).astype(BF16)))
    w_ref[...] = w
    x_ref[...] = x0
    ws, x0s = split(w), split(x0)
    mixed = [mm(split(score), ws) for score in scores]
    eye = jnp.where(iota((D, D), 0) == iota((D, D), 1), 1.0, 0.0)
    send_ref[:, :D] = eye - mm(keys_t, ws)
    send_ref[:, D : 3 * D] = mm(keys_t, x0s)
    qhats = [split((query * root - mix).T) for query, mix in zip(queries, mixed)]
    grads = [exact(ds_ref[r, :].astype(BF16)) for r in rows]
    back = [mm(qhat, grad) for qhat, grad in zip(qhats, grads)]
    send_ref[:, 3 * D :] = jnp.concatenate(back, axis=1)


def side_kernel(index_ref, sent_ref, k_ref, inv_ref, q_ref, d_ref, m_ref, z_ref, qs_ref, ds_ref):
    del sent_ref
    rows = load_heads([(q_ref, qs_ref), (d_ref, ds_ref)])
    root = places_root(index_ref[0])
    keys, inv_t = split(k_ref[...]), split(inv_ref[...].T)
    m_ref[...] = mm(inv_t, keys)
    back = []
    for head in range(2):
        score = causal_scores(qs_ref[rows[head], :], keys, root)
        back.append(mm(split(score.T), exact(ds_ref[rows[head], :].astype(BF16))))
    z_ref[...] = mm(inv_t, split(jnp.concatenate(back, axis=1)))


def then(first, second):
    step = mm(split(second[:, :D]), split(first))
    return jnp.concatenate([step[:, :D], step[:, D:] + second[:, D:]], axis=1)


def along(index_ref, size, unit):
    place = (index_ref[0] // unit) % size
    return jnp.where(index_ref[0] % 2 == 1, size - 1 - place, place)


def pair_kernel(index_ref, got_ref, own_ref, send_ref):
    down, right = index_ref[0] % 2 == 1, (index_ref[0] // 2) % 2 == 1

    def ranges(i):
        return jnp.concatenate(
            [
                jnp.where(down, got_ref[1 - i, :, :D].T, got_ref[i, :, :D]),
                jnp.where(down, got_ref[1 - i, :, 3 * D :], got_ref[i, :, D : 3 * D]),
            ],
            axis=1,
        )

    chip = then(ranges(0), ranges(1))
    left, rest = chip[:, : 2 * D], jnp.concatenate([chip[:, :D], chip[:, 2 * D :]], axis=1)
    own_ref[...] = jnp.where(right, rest, left)
    send_ref[...] = jnp.where(right, left, rest)


def chip_kernel(index_ref, own_ref, got_ref, first_ref, send_ref):
    down, right = index_ref[0] % 2 == 1, (index_ref[0] // 2) % 2 == 1
    own, other = own_ref[...], jnp.where(right, got_ref[0], got_ref[1])
    first = jnp.where(right == down, own, other)
    first_ref[...] = first
    send_ref[...] = then(first, jnp.where(right == down, other, own))


def block_kernel(index_ref, got_ref, send_ref, block_ref):
    down = index_ref[0] % 2 == 1
    first, second = [jnp.where(down, got_ref[1 - i], got_ref[i]) for i in range(2)]
    whole = then(first, second)
    block_ref[...] = whole
    send_ref[...] = whole[:, D:]


def hop_kernel(got_ref, block_ref, send_ref):
    send_ref[...] = block_ref[:, D:] + mm(split(block_ref[:, :D]), split(got_ref[...]))


def top_kernel(index_ref, first_ref, second_ref, third_ref, units_ref, chip_ref, send_ref):
    down = index_ref[0] % 2 == 1
    place = along(index_ref, 4, 8)
    got = jnp.where(
        place == 1, first_ref[...], jnp.where(place == 2, second_ref[...], jnp.where(place == 3, third_ref[...], 0.0))
    )
    unit = jnp.where(down, units_ref[1], units_ref[0])
    later = unit[:, D:] + mm(split(unit[:, :D]), split(got))
    got = jnp.where(along(index_ref, 2, 4) == 1, later, got)
    send_ref[:, :D] = got
    send_ref[:, D:] = chip_ref[:, D:] + mm(split(chip_ref[:, :D]), split(got))


def after_kernel(index_ref, pair_ref, got_ref, q_ref, d_ref, k_ref, w_ref, m_ref, x0_ref, z0_ref,
                 gk_ref, s_ref, x_ref, z_ref, qs_ref, ds_ref):
    qs_ref[...] = q_ref[...].astype(F32)
    ds_ref[...] = d_ref[...].astype(F32)
    rows = [pl.ds(head, T, stride=2) for head in range(2)]
    upper = index_ref[0] % 2 == 1
    right = (index_ref[0] // 2) % 2 == 1
    state, adjoint = [
        jnp.concatenate(
            [jnp.where(right == flip, got_ref[i, :, :D], got_ref[i, :, D:]) for i in (core, core + 2)], axis=1
        )
        for core, flip in ((0, False), (1, True))
    ]
    step = mm(
        split(jnp.where(upper, pair_ref[0, :, :D], pair_ref[1, :, :D].T)),
        split(jnp.where(upper, state, adjoint)),
    )
    state = jnp.where(upper, step + pair_ref[0, :, D : 3 * D], state)
    adjoint = jnp.where(upper, adjoint, step + pair_ref[1, :, 3 * D :])
    s_ref[...] = state
    states, adjoints = split(state), split(adjoint)
    root = places_root(index_ref[0])
    keys = split(k_ref[...])
    row, col = iota((T, T), 0), iota((T, T), 1)
    x = x0_ref[...] - mm(split(w_ref[...]), states)
    x_ref[...] = x
    xs = split(x)
    z = z0_ref[...] + mm(split(m_ref[...]), adjoints)
    z_ref[...] = z
    zs = split(z)
    parts = [slice(head * D, (head + 1) * D) for head in range(2)]
    queries = [exact(qs_ref[r, :].astype(BF16)) for r in rows]
    grads = [exact(ds_ref[r, :].astype(BF16)) for r in rows]
    edge = mm(zs, xs, (1, 1))
    mixed = [mm(grad, tuple(s[:, part] for s in xs), (1, 1)) for grad, part in zip(grads, parts)]
    gk = mm(xs, adjoints, (1, 1)) - 2.0 * mm(zs, states, (1, 1))
    edge = jnp.where(row > col, edge, 0.0)
    mixed = [split((jnp.where(row >= col, mix, 0.0) * root).T) for mix in mixed]
    last = [mm(mix, query) for mix, query in zip(mixed, queries)]
    gk = gk - 2.0 * mm(split(edge + edge.T), keys) + last[0] + last[1]
    gk_ref[...] = gk


def rest_kernel(index_ref, q_ref, d_ref, k_ref, s_ref, x_ref, z_ref, out_ref, gq_ref, gv_ref, qs_ref, ds_ref,
                os_ref, gs_ref, zs_ref):
    qs_ref[...] = q_ref[...].astype(F32)
    ds_ref[...] = d_ref[...].astype(F32)
    rows = [pl.ds(head, T, stride=2) for head in range(2)]
    root = places_root(index_ref[0])
    keys = split(k_ref[...])
    row, col = iota((T, T), 0), iota((T, T), 1)
    states, xs = split(s_ref[...]), split(x_ref[...])
    for head in range(2):
        part = slice(head * D, (head + 1) * D)
        head_states, head_xs = tuple(s[:, part] for s in states), tuple(s[:, part] for s in xs)
        query = exact(qs_ref[rows[head], :].astype(BF16))
        grad = exact(ds_ref[rows[head], :].astype(BF16))
        score = jnp.where(row >= col, mm(query, keys, (1, 1)), 0.0)
        os_ref[rows[head], :] = root * (mm(query, head_states) + mm(split(score), head_xs))
        mix = jnp.where(row >= col, mm(grad, head_xs, (1, 1)), 0.0)
        gs_ref[rows[head], :] = root * (mm(grad, head_states, (1, 1)) + mm(split(mix), keys))
        zs_ref[rows[head], :] = z_ref[:, part]
    out_ref[...] = os_ref[...].astype(BF16)
    gq_ref[...] = gs_ref[...].astype(BF16)
    gv_ref[...] = zs_ref[...].astype(BF16)


def sum_kernel(got_ref, out_ref):
    out_ref[...] = jnp.broadcast_to(jnp.sum(got_ref[...], axis=0, keepdims=True), out_ref.shape)


def key_kernel(got_ref, k_ref, norm_ref, out_ref):
    total, key = got_ref[...], k_ref[...]
    along = jnp.sum(total * key, axis=1, keepdims=True)
    out_ref[...] = ((total - key * along) * norm_ref[...]).astype(BF16)


def call(kernel, outs, *operands, scratch=(), scalars=1, cost=None):
    spaces = [pltpu.SMEM] * scalars + [pltpu.VMEM] * (len(operands) - scalars)
    single = not isinstance(outs, list)
    shapes = [outs] if single else outs
    result = pl.pallas_call(
        kernel,
        out_shape=[jax.ShapeDtypeStruct(*s) for s in shapes],
        in_specs=[pl.BlockSpec(memory_space=space) for space in spaces],
        out_specs=[pl.BlockSpec(memory_space=pltpu.VMEM)] * len(shapes),
        scratch_shapes=list(scratch),
        compiler_params=pltpu.CompilerParams(vmem_limit_bytes=VMEM_LIMIT),
        cost_estimate=cost,
    )(*operands)
    return result[0] if single else result


def exchange(x, groups):
    return lax.all_gather(x, "seq", axis_index_groups=groups)


def near(*offsets):
    groups, taken = [], set()
    for i in range(PARTS):
        if i not in taken:
            groups.append([i + offset for offset in offsets])
            taken.update(groups[-1])
    return groups


def hop(x, place):
    up = [(8 * place + i, 8 * place + i + 8) for i in range(0, 8, 2)]
    return lax.ppermute(x, "seq", up + [(PARTS - 1 - a, PARTS - 1 - b) for a, b in up])


def shards(queries, raw_keys, values, cotangent):
    index = lax.axis_index("seq").astype(jnp.int32).reshape(1)
    q = queries.reshape(2 * T, D)
    v = values.reshape(2 * T, D)
    d = cotangent.reshape(2 * T, D)
    wide = pltpu.VMEM((2 * T, D), F32)
    key, norm, inv = call(
        keys_kernel, [((T, D), F32), ((T, D), F32), ((T, T), F32)], raw_keys, scalars=0, cost=LONG
    )
    send, w, x0 = call(
        before_kernel,
        [((D, 5 * D), F32), ((T, D), F32), ((T, 2 * D), F32)],
        index, key, inv, q, v, d,
        scratch=[wide] * 3,
    )
    pair = exchange(send, near(0, 1))
    own, send = call(pair_kernel, [((D, 2 * D), F32)] * 2, index, pair)
    chip, send = call(chip_kernel, [((D, 2 * D), F32)] * 2, index, own, exchange(send, near(0, 2)))
    units = exchange(send, near(0, 4))
    send, block = call(block_kernel, [((D, D), F32), ((D, 2 * D), F32)], index, units)
    first = hop(send, 0)
    m, z0 = call(
        side_kernel,
        [((T, D), F32), ((T, 2 * D), F32)],
        index, send, key, inv, q, d,
        scratch=[wide] * 2,
        cost=SHORT,
    )
    send = call(hop_kernel, ((D, D), F32), first, block, scalars=0)
    second = hop(send, 1)
    send = call(hop_kernel, ((D, D), F32), second, block, scalars=0)
    third = hop(send, 2)
    send = call(top_kernel, ((D, 2 * D), F32), index, first, second, third, units, chip)
    got = exchange(send, near(0, 1, 2, 3))
    gk, state, x, z = call(
        after_kernel,
        [((T, D), F32), ((D, 2 * D), F32), ((T, 2 * D), F32), ((T, 2 * D), F32)],
        index, pair, got, q, d, key, w, m, x0, z0,
        scratch=[wide] * 2,
    )
    peers = lax.axis_size("head")
    pieces = lax.all_to_all(gk.reshape(peers, T // peers, D), "head", 0, 0)
    out, gq, gv = call(
        rest_kernel,
        [((2 * T, D), BF16)] * 3,
        index, q, d, key, state, x, z,
        scratch=[wide] * 5,
        cost=LONG,
    )
    totals = call(sum_kernel, ((peers, T // peers, D), F32), pieces, scalars=0)
    total = lax.all_to_all(totals, "head", 0, 0).reshape(T, D)
    gkey = call(key_kernel, ((T, D), BF16), total, key, norm, scalars=0)
    shape = queries.shape
    return out.reshape(shape), gq.reshape(shape), gkey, gv.reshape(shape)


def solution(mesh):
    split_both = P("seq", "head", None)
    keys_only = P("seq", None)
    return jax.shard_map(
        shards,
        mesh=mesh,
        in_specs=(split_both, keys_only, split_both, split_both),
        out_specs=(split_both, split_both, keys_only, split_both),
        check_vma=False,
    )
```

```python
import jax
import jax.numpy as jnp
from jax import lax
from jax.experimental import pallas as pl
from jax.experimental.pallas import tpu as pltpu
from jax.sharding import PartitionSpec as P

T = 256
PARTS = 32
D = 128
F32 = jnp.float32
BF16 = jnp.bfloat16
VMEM_LIMIT = 48 * 1024 * 1024
SHORT = pl.CostEstimate(flops=500000000, bytes_accessed=1000000, transcendentals=0)
LONG = pl.CostEstimate(flops=4000000000, bytes_accessed=4000000, transcendentals=0)


def split(x):
    high = x.astype(BF16)
    return high, (x - high.astype(F32)).astype(BF16)


def exact(x):
    return x, None


def mm(a, b, over=(1, 0)):
    ca, cb = over
    terms = [(a[0], b[0])]
    if b[1] is not None:
        terms.append((a[0], b[1]))
    if a[1] is not None:
        terms.append((a[1], b[0]))
    left = jnp.concatenate([t[0] for t in terms], axis=ca)
    right = jnp.concatenate([t[1] for t in terms], axis=cb)
    return lax.dot_general(left, right, (((ca,), (cb,)), ((), ())), preferred_element_type=F32)


def iota(shape, dim):
    return lax.broadcasted_iota(jnp.int32, shape, dim)


def inverses(lowers, size):
    row, col = iota((size, size), 0), iota((size, size), 1)
    level = row ^ col

    def part(low, high):
        return [jnp.where((level >= low) & (level < high), lower, 0.0) for lower in lowers]

    edges = part(1, 4)
    starts = [jnp.where(row == col, 1.0, -edge) for edge in edges]
    edges = [split(edge) for edge in edges]
    squares = [split(mm(edge, edge)) for edge in edges]
    invs = [start + mm(square, split(start)) for start, square in zip(starts, squares)]
    step = 4
    while step < size:
        pairs = [split(inv) for inv in invs]
        if 4 * step <= size:
            edges = [split(mm(pair, split(edge))) for pair, edge in zip(pairs, part(step, 4 * step))]
            starts = [mm(edge, pair) for edge, pair in zip(edges, pairs)]
            squares = [mm(edge, edge) for edge in edges]
            starts = [inv - start for inv, start in zip(invs, starts)]
            invs = [start + mm(split(square), split(start)) for start, square in zip(starts, squares)]
            step *= 4
        else:
            edges = [split(mm(split(edge), pair)) for pair, edge in zip(pairs, part(step, 2 * step))]
            invs = [inv - mm(pair, edge) for inv, pair, edge in zip(invs, pairs, edges)]
            step *= 2
    return invs


def places_root(index):
    places = (index % PARTS * T + iota((T, 1), 0) + 1).astype(F32)
    return 1.0 / jnp.sqrt(places)


def keys_kernel(raw_ref, k_ref, norm_ref, inv_ref):
    raw = raw_ref[...].astype(F32)
    norm = 1.0 / jnp.sqrt(jnp.sum(raw * raw, axis=1, keepdims=True) + 1e-06)
    key = raw * norm
    k_ref[...] = key
    norm_ref[...] = jnp.broadcast_to(norm, (T, D))
    keys = split(key)
    gram = mm(keys, keys, (1, 1))
    row, col = iota((T, T), 0), iota((T, T), 1)
    lower = jnp.where(row > col, 2.0 * gram, 0.0)
    half = T // 2
    first, second = inverses([lower[:half, :half], lower[half:, half:]], half)
    corner = -mm(split(second), split(mm(split(lower[half:, :half]), split(first))))
    inv_ref[:half, :half] = first
    inv_ref[:half, half:] = jnp.zeros((half, half), F32)
    inv_ref[half:, :half] = corner
    inv_ref[half:, half:] = second


def load_heads(pairs):
    for source, room in pairs:
        room[...] = source[...].astype(F32)
    return [pl.ds(head, T, stride=2) for head in range(2)]


def causal_scores(query, keys, root):
    row, col = iota((T, T), 0), iota((T, T), 1)
    return jnp.where(row >= col, mm(exact(query.astype(BF16)), keys, (1, 1)), 0.0) * root


def before_kernel(index_ref, k_ref, inv_ref, q_ref, v_ref, d_ref, send_ref, w_ref, x_ref, qs_ref, vs_ref, ds_ref):
    rows = load_heads([(q_ref, qs_ref), (v_ref, vs_ref), (d_ref, ds_ref)])
    root = places_root(index_ref[0])
    key = k_ref[...]
    keys, invs, keys_t = split(key), split(inv_ref[...]), split(key.T)
    queries = [qs_ref[r, :] for r in rows]
    scores = [causal_scores(query, keys, root) for query in queries]
    w = 2.0 * mm(invs, keys)
    x0 = mm(invs, exact(jnp.concatenate([vs_ref[r, :] for r in rows], axis=1).astype(BF16)))
    w_ref[...] = w
    x_ref[...] = x0
    ws, x0s = split(w), split(x0)
    mixed = [mm(split(score), ws) for score in scores]
    eye = jnp.where(iota((D, D), 0) == iota((D, D), 1), 1.0, 0.0)
    send_ref[:, :D] = eye - mm(keys_t, ws)
    send_ref[:, D : 3 * D] = mm(keys_t, x0s)
    qhats = [split((query * root - mix).T) for query, mix in zip(queries, mixed)]
    grads = [exact(ds_ref[r, :].astype(BF16)) for r in rows]
    back = [mm(qhat, grad) for qhat, grad in zip(qhats, grads)]
    send_ref[:, 3 * D :] = jnp.concatenate(back, axis=1)


def side_kernel(index_ref, sent_ref, k_ref, inv_ref, q_ref, d_ref, m_ref, z_ref, qs_ref, ds_ref):
    del sent_ref
    rows = load_heads([(q_ref, qs_ref), (d_ref, ds_ref)])
    root = places_root(index_ref[0])
    keys, inv_t = split(k_ref[...]), split(inv_ref[...].T)
    m_ref[...] = mm(inv_t, keys)
    back = []
    for head in range(2):
        score = causal_scores(qs_ref[rows[head], :], keys, root)
        back.append(mm(split(score.T), exact(ds_ref[rows[head], :].astype(BF16))))
    z_ref[...] = mm(inv_t, split(jnp.concatenate(back, axis=1)))


def then(first, second):
    step = mm(split(second[:, :D]), split(first))
    return jnp.concatenate([step[:, :D], step[:, D:] + second[:, D:]], axis=1)


def along(index_ref, size, unit):
    place = (index_ref[0] // unit) % size
    return jnp.where(index_ref[0] % 2 == 1, size - 1 - place, place)


def pair_kernel(index_ref, got_ref, own_ref, send_ref):
    down, right = index_ref[0] % 2 == 1, (index_ref[0] // 2) % 2 == 1

    def ranges(i):
        return jnp.concatenate(
            [
                jnp.where(down, got_ref[1 - i, :, :D].T, got_ref[i, :, :D]),
                jnp.where(down, got_ref[1 - i, :, 3 * D :], got_ref[i, :, D : 3 * D]),
            ],
            axis=1,
        )

    chip = then(ranges(0), ranges(1))
    left, rest = chip[:, : 2 * D], jnp.concatenate([chip[:, :D], chip[:, 2 * D :]], axis=1)
    own_ref[...] = jnp.where(right, rest, left)
    send_ref[...] = jnp.where(right, left, rest)


def chip_kernel(index_ref, own_ref, got_ref, first_ref, send_ref):
    down, right = index_ref[0] % 2 == 1, (index_ref[0] // 2) % 2 == 1
    own, other = own_ref[...], jnp.where(right, got_ref[0], got_ref[1])
    first = jnp.where(right == down, own, other)
    first_ref[...] = first
    send_ref[...] = then(first, jnp.where(right == down, other, own))


def block_kernel(index_ref, got_ref, send_ref, block_ref):
    down = index_ref[0] % 2 == 1
    first, second = [jnp.where(down, got_ref[1 - i], got_ref[i]) for i in range(2)]
    whole = then(first, second)
    block_ref[...] = whole
    send_ref[...] = whole[:, D:]


def hop_kernel(got_ref, block_ref, send_ref):
    send_ref[...] = block_ref[:, D:] + mm(split(block_ref[:, :D]), split(got_ref[...]))


def top_kernel(index_ref, first_ref, second_ref, third_ref, units_ref, chip_ref, send_ref):
    down = index_ref[0] % 2 == 1
    place = along(index_ref, 4, 8)
    got = jnp.where(
        place == 1, first_ref[...], jnp.where(place == 2, second_ref[...], jnp.where(place == 3, third_ref[...], 0.0))
    )
    unit = jnp.where(down, units_ref[1], units_ref[0])
    later = unit[:, D:] + mm(split(unit[:, :D]), split(got))
    got = jnp.where(along(index_ref, 2, 4) == 1, later, got)
    send_ref[:, :D] = got
    send_ref[:, D:] = chip_ref[:, D:] + mm(split(chip_ref[:, :D]), split(got))


def after_kernel(index_ref, pair_ref, got_ref, q_ref, d_ref, k_ref, w_ref, m_ref, x0_ref, z0_ref,
                 gk_ref, s_ref, x_ref, z_ref, qs_ref, ds_ref):
    qs_ref[...] = q_ref[...].astype(F32)
    ds_ref[...] = d_ref[...].astype(F32)
    rows = [pl.ds(head, T, stride=2) for head in range(2)]
    upper = index_ref[0] % 2 == 1
    right = (index_ref[0] // 2) % 2 == 1
    state, adjoint = [
        jnp.concatenate(
            [jnp.where(right == flip, got_ref[i, :, :D], got_ref[i, :, D:]) for i in (core, core + 2)], axis=1
        )
        for core, flip in ((0, False), (1, True))
    ]
    step = mm(
        split(jnp.where(upper, pair_ref[0, :, :D], pair_ref[1, :, :D].T)),
        split(jnp.where(upper, state, adjoint)),
    )
    state = jnp.where(upper, step + pair_ref[0, :, D : 3 * D], state)
    adjoint = jnp.where(upper, adjoint, step + pair_ref[1, :, 3 * D :])
    s_ref[...] = state
    states, adjoints = split(state), split(adjoint)
    across = 1.0 / jnp.sqrt((index_ref[0] % PARTS * T + iota((1, T), 1) + 1).astype(F32))
    keys = split(k_ref[...])
    row, col = iota((T, T), 0), iota((T, T), 1)
    x = x0_ref[...] - mm(split(w_ref[...]), states)
    x_ref[...] = x
    xs = split(x)
    z = z0_ref[...] + mm(split(m_ref[...]), adjoints)
    z_ref[...] = z
    zs = split(z)
    parts = [slice(head * D, (head + 1) * D) for head in range(2)]
    queries = [exact(qs_ref[r, :].astype(BF16)) for r in rows]
    grads = [exact(ds_ref[r, :].astype(BF16)) for r in rows]
    edge = mm(zs, xs, (1, 1))
    mixed = [mm(tuple(s[:, part] for s in xs), grad, (1, 1)) for grad, part in zip(grads, parts)]
    gk = mm(xs, adjoints, (1, 1)) - 2.0 * mm(zs, states, (1, 1))
    edge = jnp.where(row > col, edge, 0.0)
    mixed = [split(jnp.where(col >= row, mix, 0.0) * across) for mix in mixed]
    last = [mm(mix, query) for mix, query in zip(mixed, queries)]
    gk = gk - 2.0 * mm(split(edge + edge.T), keys) + last[0] + last[1]
    gk_ref[...] = gk


def rest_kernel(index_ref, q_ref, d_ref, k_ref, s_ref, x_ref, z_ref, out_ref, gq_ref, gv_ref, qs_ref, ds_ref,
                os_ref, gs_ref, zs_ref):
    qs_ref[...] = q_ref[...].astype(F32)
    ds_ref[...] = d_ref[...].astype(F32)
    rows = [pl.ds(head, T, stride=2) for head in range(2)]
    root = places_root(index_ref[0])
    keys = split(k_ref[...])
    row, col = iota((T, T), 0), iota((T, T), 1)
    states, xs = split(s_ref[...]), split(x_ref[...])
    for head in range(2):
        part = slice(head * D, (head + 1) * D)
        head_states, head_xs = tuple(s[:, part] for s in states), tuple(s[:, part] for s in xs)
        query = exact(qs_ref[rows[head], :].astype(BF16))
        grad = exact(ds_ref[rows[head], :].astype(BF16))
        score = jnp.where(row >= col, mm(query, keys, (1, 1)), 0.0)
        os_ref[rows[head], :] = root * (mm(query, head_states) + mm(split(score), head_xs))
        mix = jnp.where(row >= col, mm(grad, head_xs, (1, 1)), 0.0)
        gs_ref[rows[head], :] = root * (mm(grad, head_states, (1, 1)) + mm(split(mix), keys))
        zs_ref[rows[head], :] = z_ref[:, part]
    out_ref[...] = os_ref[...].astype(BF16)
    gq_ref[...] = gs_ref[...].astype(BF16)
    gv_ref[...] = zs_ref[...].astype(BF16)


def sum_kernel(index_ref, got_ref, k_ref, norm_ref, out_ref):
    count = got_ref.shape[1]
    rows = pl.ds(pl.multiple_of((index_ref[0] // PARTS) * count, count), count)
    total, key = jnp.sum(got_ref[...], axis=0), k_ref[rows, :]
    total = (total - key * jnp.sum(total * key, axis=1, keepdims=True)) * norm_ref[rows, :]
    out_ref[...] = jnp.broadcast_to(total[None], out_ref.shape)


def key_kernel(got_ref, out_ref):
    out_ref[...] = got_ref[...].astype(BF16)


def call(kernel, outs, *operands, scratch=(), scalars=1, cost=None):
    spaces = [pltpu.SMEM] * scalars + [pltpu.VMEM] * (len(operands) - scalars)
    single = not isinstance(outs, list)
    shapes = [outs] if single else outs
    result = pl.pallas_call(
        kernel,
        out_shape=[jax.ShapeDtypeStruct(*s) for s in shapes],
        in_specs=[pl.BlockSpec(memory_space=space) for space in spaces],
        out_specs=[pl.BlockSpec(memory_space=pltpu.VMEM)] * len(shapes),
        scratch_shapes=list(scratch),
        compiler_params=pltpu.CompilerParams(vmem_limit_bytes=VMEM_LIMIT),
        cost_estimate=cost,
    )(*operands)
    return result[0] if single else result


def exchange(x, groups):
    return lax.all_gather(x, "seq", axis_index_groups=groups)


def near(*offsets):
    groups, taken = [], set()
    for i in range(PARTS):
        if i not in taken:
            groups.append([i + offset for offset in offsets])
            taken.update(groups[-1])
    return groups


def hop(x, place):
    up = [(8 * place + i, 8 * place + i + 8) for i in range(0, 8, 2)]
    return lax.ppermute(x, "seq", up + [(PARTS - 1 - a, PARTS - 1 - b) for a, b in up])


def shards(queries, raw_keys, values, cotangent):
    index = (lax.axis_index("seq") + PARTS * lax.axis_index("head")).astype(jnp.int32).reshape(1)
    q = queries.reshape(2 * T, D)
    v = values.reshape(2 * T, D)
    d = cotangent.reshape(2 * T, D)
    wide = pltpu.VMEM((2 * T, D), F32)
    key, norm, inv = call(
        keys_kernel, [((T, D), F32), ((T, D), F32), ((T, T), F32)], raw_keys, scalars=0, cost=LONG
    )
    send, w, x0 = call(
        before_kernel,
        [((D, 5 * D), F32), ((T, D), F32), ((T, 2 * D), F32)],
        index, key, inv, q, v, d,
        scratch=[wide] * 3,
    )
    pair = exchange(send, near(0, 1))
    own, send = call(pair_kernel, [((D, 2 * D), F32)] * 2, index, pair)
    chip, send = call(chip_kernel, [((D, 2 * D), F32)] * 2, index, own, exchange(send, near(0, 2)))
    units = exchange(send, near(0, 4))
    send, block = call(block_kernel, [((D, D), F32), ((D, 2 * D), F32)], index, units)
    first = hop(send, 0)
    m, z0 = call(
        side_kernel,
        [((T, D), F32), ((T, 2 * D), F32)],
        index, send, key, inv, q, d,
        scratch=[wide] * 2,
        cost=SHORT,
    )
    send = call(hop_kernel, ((D, D), F32), first, block, scalars=0)
    second = hop(send, 1)
    send = call(hop_kernel, ((D, D), F32), second, block, scalars=0)
    third = hop(send, 2)
    send = call(top_kernel, ((D, 2 * D), F32), index, first, second, third, units, chip)
    got = exchange(send, near(0, 1, 2, 3))
    gk, state, x, z = call(
        after_kernel,
        [((T, D), F32), ((D, 2 * D), F32), ((T, 2 * D), F32), ((T, 2 * D), F32)],
        index, pair, got, q, d, key, w, m, x0, z0,
        scratch=[wide] * 2,
    )
    peers = lax.axis_size("head")
    pieces = lax.all_to_all(gk.reshape(peers, T // peers, D), "head", 0, 0)
    out, gq, gv = call(
        rest_kernel,
        [((2 * T, D), BF16)] * 3,
        index, q, d, key, state, x, z,
        scratch=[wide] * 5,
        cost=LONG,
    )
    totals = call(sum_kernel, ((peers, T // peers, D), F32), index, pieces, key, norm)
    total = lax.all_to_all(totals, "head", 0, 0).reshape(T, D)
    gkey = call(key_kernel, ((T, D), BF16), total, scalars=0)
    shape = queries.shape
    return out.reshape(shape), gq.reshape(shape), gkey, gv.reshape(shape)


def solution(mesh):
    split_both = P("seq", "head", None)
    keys_only = P("seq", None)
    return jax.shard_map(
        shards,
        mesh=mesh,
        in_specs=(split_both, keys_only, split_both, split_both),
        out_specs=(split_both, split_both, keys_only, split_both),
        check_vma=False,
    )
```

```python
import jax
import jax.numpy as jnp
from jax import lax
from jax.experimental import pallas as pl
from jax.experimental.pallas import tpu as pltpu
from jax.sharding import PartitionSpec as P

T = 256
PARTS = 32
D = 128
F32 = jnp.float32
BF16 = jnp.bfloat16
VMEM_LIMIT = 48 * 1024 * 1024
SHORT = pl.CostEstimate(flops=500000000, bytes_accessed=1000000, transcendentals=0)
LONG = pl.CostEstimate(flops=4000000000, bytes_accessed=4000000, transcendentals=0)


def split(x):
    high = x.astype(BF16)
    return high, (x - high.astype(F32)).astype(BF16)


def exact(x):
    return x, None


def mm(a, b, over=(1, 0)):
    ca, cb = over
    terms = [(a[0], b[0])]
    if b[1] is not None:
        terms.append((a[0], b[1]))
    if a[1] is not None:
        terms.append((a[1], b[0]))
    left = jnp.concatenate([t[0] for t in terms], axis=ca)
    right = jnp.concatenate([t[1] for t in terms], axis=cb)
    return lax.dot_general(left, right, (((ca,), (cb,)), ((), ())), preferred_element_type=F32)


def iota(shape, dim):
    return lax.broadcasted_iota(jnp.int32, shape, dim)


def inverses(lowers, size):
    row, col = iota((size, size), 0), iota((size, size), 1)
    level = row ^ col

    def part(low, high):
        return [jnp.where((level >= low) & (level < high), lower, 0.0) for lower in lowers]

    edges = part(1, 4)
    starts = [jnp.where(row == col, 1.0, -edge) for edge in edges]
    edges = [split(edge) for edge in edges]
    squares = [split(mm(edge, edge)) for edge in edges]
    invs = [start + mm(square, split(start)) for start, square in zip(starts, squares)]
    step = 4
    while step < size:
        pairs = [split(inv) for inv in invs]
        if 4 * step <= size:
            edges = [split(mm(pair, split(edge))) for pair, edge in zip(pairs, part(step, 4 * step))]
            starts = [mm(edge, pair) for edge, pair in zip(edges, pairs)]
            squares = [mm(edge, edge) for edge in edges]
            starts = [inv - start for inv, start in zip(invs, starts)]
            invs = [start + mm(split(square), split(start)) for start, square in zip(starts, squares)]
            step *= 4
        else:
            edges = [split(mm(split(edge), pair)) for pair, edge in zip(pairs, part(step, 2 * step))]
            invs = [inv - mm(pair, edge) for inv, pair, edge in zip(invs, pairs, edges)]
            step *= 2
    return invs


def places_root(index):
    places = (index % PARTS * T + iota((T, 1), 0) + 1).astype(F32)
    return 1.0 / jnp.sqrt(places)


def keys_kernel(raw_ref, k_ref, norm_ref, inv_ref):
    raw = raw_ref[...].astype(F32)
    norm = 1.0 / jnp.sqrt(jnp.sum(raw * raw, axis=1, keepdims=True) + 1e-06)
    key = raw * norm
    k_ref[...] = key
    norm_ref[...] = jnp.broadcast_to(norm, (T, D))
    keys = split(key)
    gram = mm(keys, keys, (1, 1))
    row, col = iota((T, T), 0), iota((T, T), 1)
    lower = jnp.where(row > col, 2.0 * gram, 0.0)
    half = T // 2
    first, second = inverses([lower[:half, :half], lower[half:, half:]], half)
    corner = -mm(split(second), split(mm(split(lower[half:, :half]), split(first))))
    inv_ref[:half, :half] = first
    inv_ref[:half, half:] = jnp.zeros((half, half), F32)
    inv_ref[half:, :half] = corner
    inv_ref[half:, half:] = second


def load_heads(pairs):
    for source, room in pairs:
        room[...] = source[...].astype(F32)
    return [pl.ds(head, T, stride=2) for head in range(2)]


def causal_scores(query, keys, root):
    row, col = iota((T, T), 0), iota((T, T), 1)
    return jnp.where(row >= col, mm(exact(query.astype(BF16)), keys, (1, 1)), 0.0) * root


def before_kernel(index_ref, k_ref, inv_ref, q_ref, v_ref, d_ref, send_ref, w_ref, x_ref, qs_ref, vs_ref, ds_ref):
    rows = load_heads([(q_ref, qs_ref), (v_ref, vs_ref), (d_ref, ds_ref)])
    root = places_root(index_ref[0])
    key = k_ref[...]
    keys, invs, keys_t = split(key), split(inv_ref[...]), split(key.T)
    queries = [qs_ref[r, :] for r in rows]
    w = 2.0 * mm(invs, keys)
    scores = [causal_scores(query, keys, root) for query in queries]
    x0 = mm(invs, exact(jnp.concatenate([vs_ref[r, :] for r in rows], axis=1).astype(BF16)))
    w_ref[...] = w
    x_ref[...] = x0
    ws, x0s = split(w), split(x0)
    mixed = [mm(split(score), ws) for score in scores]
    eye = jnp.where(iota((D, D), 0) == iota((D, D), 1), 1.0, 0.0)
    send_ref[:, :D] = eye - mm(keys_t, ws)
    send_ref[:, D : 3 * D] = mm(keys_t, x0s)
    qhats = [split((query * root - mix).T) for query, mix in zip(queries, mixed)]
    grads = [exact(ds_ref[r, :].astype(BF16)) for r in rows]
    back = [mm(qhat, grad) for qhat, grad in zip(qhats, grads)]
    send_ref[:, 3 * D :] = jnp.concatenate(back, axis=1)


def side_kernel(index_ref, sent_ref, k_ref, inv_ref, q_ref, d_ref, m_ref, z_ref, qs_ref, ds_ref):
    del sent_ref
    rows = load_heads([(q_ref, qs_ref), (d_ref, ds_ref)])
    root = places_root(index_ref[0])
    keys, inv_t = split(k_ref[...]), split(inv_ref[...].T)
    m_ref[...] = mm(inv_t, keys)
    back = []
    for head in range(2):
        score = causal_scores(qs_ref[rows[head], :], keys, root)
        back.append(mm(split(score.T), exact(ds_ref[rows[head], :].astype(BF16))))
    z_ref[...] = mm(inv_t, split(jnp.concatenate(back, axis=1)))


def then(first, second):
    step = mm(split(second[:, :D]), split(first))
    return jnp.concatenate([step[:, :D], step[:, D:] + second[:, D:]], axis=1)


def along(index_ref, size, unit):
    place = (index_ref[0] // unit) % size
    return jnp.where(index_ref[0] % 2 == 1, size - 1 - place, place)


def pair_kernel(index_ref, got_ref, own_ref, send_ref):
    down, right = index_ref[0] % 2 == 1, (index_ref[0] // 2) % 2 == 1

    def ranges(i):
        return jnp.concatenate(
            [
                jnp.where(down, got_ref[1 - i, :, :D].T, got_ref[i, :, :D]),
                jnp.where(down, got_ref[1 - i, :, 3 * D :], got_ref[i, :, D : 3 * D]),
            ],
            axis=1,
        )

    chip = then(ranges(0), ranges(1))
    left, rest = chip[:, : 2 * D], jnp.concatenate([chip[:, :D], chip[:, 2 * D :]], axis=1)
    own_ref[...] = jnp.where(right, rest, left)
    send_ref[...] = jnp.where(right, left, rest)


def chip_kernel(index_ref, own_ref, got_ref, first_ref, send_ref):
    down, right = index_ref[0] % 2 == 1, (index_ref[0] // 2) % 2 == 1
    own, other = own_ref[...], jnp.where(right, got_ref[0], got_ref[1])
    first = jnp.where(right == down, own, other)
    first_ref[...] = first
    send_ref[...] = then(first, jnp.where(right == down, other, own))


def block_kernel(index_ref, got_ref, send_ref, block_ref):
    down = index_ref[0] % 2 == 1
    first, second = [jnp.where(down, got_ref[1 - i], got_ref[i]) for i in range(2)]
    whole = then(first, second)
    block_ref[...] = whole
    send_ref[...] = whole[:, D:]


def hop_kernel(got_ref, block_ref, send_ref):
    send_ref[...] = block_ref[:, D:] + mm(split(block_ref[:, :D]), split(got_ref[...]))


def top_kernel(index_ref, first_ref, second_ref, third_ref, units_ref, chip_ref, send_ref):
    down = index_ref[0] % 2 == 1
    place = along(index_ref, 4, 8)
    got = jnp.where(
        place == 1, first_ref[...], jnp.where(place == 2, second_ref[...], jnp.where(place == 3, third_ref[...], 0.0))
    )
    unit = jnp.where(down, units_ref[1], units_ref[0])
    later = unit[:, D:] + mm(split(unit[:, :D]), split(got))
    got = jnp.where(along(index_ref, 2, 4) == 1, later, got)
    send_ref[:, :D] = got
    send_ref[:, D:] = chip_ref[:, D:] + mm(split(chip_ref[:, :D]), split(got))


def after_kernel(index_ref, pair_ref, got_ref, q_ref, d_ref, k_ref, w_ref, m_ref, x0_ref, z0_ref,
                 gk_ref, s_ref, x_ref, z_ref, qs_ref, ds_ref):
    qs_ref[...] = q_ref[...].astype(F32)
    ds_ref[...] = d_ref[...].astype(F32)
    rows = [pl.ds(head, T, stride=2) for head in range(2)]
    upper = index_ref[0] % 2 == 1
    right = (index_ref[0] // 2) % 2 == 1
    state, adjoint = [
        jnp.concatenate(
            [jnp.where(right == flip, got_ref[i, :, :D], got_ref[i, :, D:]) for i in (core, core + 2)], axis=1
        )
        for core, flip in ((0, False), (1, True))
    ]
    step = mm(
        split(jnp.where(upper, pair_ref[0, :, :D], pair_ref[1, :, :D].T)),
        split(jnp.where(upper, state, adjoint)),
    )
    state = jnp.where(upper, step + pair_ref[0, :, D : 3 * D], state)
    adjoint = jnp.where(upper, adjoint, step + pair_ref[1, :, 3 * D :])
    s_ref[...] = state
    states, adjoints = split(state), split(adjoint)
    across = 1.0 / jnp.sqrt((index_ref[0] % PARTS * T + iota((1, T), 1) + 1).astype(F32))
    keys = split(k_ref[...])
    row, col = iota((T, T), 0), iota((T, T), 1)
    x = x0_ref[...] - mm(split(w_ref[...]), states)
    x_ref[...] = x
    xs = split(x)
    z = z0_ref[...] + mm(split(m_ref[...]), adjoints)
    z_ref[...] = z
    zs = split(z)
    parts = [slice(head * D, (head + 1) * D) for head in range(2)]
    queries = [exact(qs_ref[r, :].astype(BF16)) for r in rows]
    grads = [exact(ds_ref[r, :].astype(BF16)) for r in rows]
    edge = mm(zs, xs, (1, 1))
    mixed = [mm(tuple(s[:, part] for s in xs), grad, (1, 1)) for grad, part in zip(grads, parts)]
    gk = mm(xs, adjoints, (1, 1)) - 2.0 * mm(zs, states, (1, 1))
    edge = jnp.where(row > col, edge, 0.0)
    mixed = [split(jnp.where(col >= row, mix, 0.0) * across) for mix in mixed]
    last = [mm(mix, query) for mix, query in zip(mixed, queries)]
    gk = gk - 2.0 * mm(split(edge + edge.T), keys) + last[0] + last[1]
    gk_ref[...] = gk


def rest_kernel(index_ref, q_ref, d_ref, k_ref, s_ref, x_ref, z_ref, out_ref, gq_ref, gv_ref, qs_ref, ds_ref,
                os_ref, gs_ref, zs_ref):
    qs_ref[...] = q_ref[...].astype(F32)
    ds_ref[...] = d_ref[...].astype(F32)
    rows = [pl.ds(head, T, stride=2) for head in range(2)]
    root = places_root(index_ref[0])
    keys = split(k_ref[...])
    row, col = iota((T, T), 0), iota((T, T), 1)
    states, xs = split(s_ref[...]), split(x_ref[...])
    for head in range(2):
        part = slice(head * D, (head + 1) * D)
        head_states, head_xs = tuple(s[:, part] for s in states), tuple(s[:, part] for s in xs)
        query = exact(qs_ref[rows[head], :].astype(BF16))
        grad = exact(ds_ref[rows[head], :].astype(BF16))
        score = jnp.where(row >= col, mm(query, keys, (1, 1)), 0.0)
        os_ref[rows[head], :] = root * (mm(query, head_states) + mm(split(score), head_xs))
        mix = jnp.where(row >= col, mm(grad, head_xs, (1, 1)), 0.0)
        gs_ref[rows[head], :] = root * (mm(grad, head_states, (1, 1)) + mm(split(mix), keys))
        zs_ref[rows[head], :] = z_ref[:, part]
    out_ref[...] = os_ref[...].astype(BF16)
    gq_ref[...] = gs_ref[...].astype(BF16)
    gv_ref[...] = zs_ref[...].astype(BF16)


def sum_kernel(index_ref, got_ref, k_ref, norm_ref, out_ref):
    count = got_ref.shape[1]
    rows = pl.ds(pl.multiple_of((index_ref[0] // PARTS) * count, count), count)
    total, key = jnp.sum(got_ref[...], axis=0), k_ref[rows, :]
    total = (total - key * jnp.sum(total * key, axis=1, keepdims=True)) * norm_ref[rows, :]
    out_ref[...] = jnp.broadcast_to(total[None], out_ref.shape)


def key_kernel(got_ref, out_ref):
    out_ref[...] = got_ref[...].astype(BF16)


def call(kernel, outs, *operands, scratch=(), scalars=1, cost=None):
    spaces = [pltpu.SMEM] * scalars + [pltpu.VMEM] * (len(operands) - scalars)
    single = not isinstance(outs, list)
    shapes = [outs] if single else outs
    result = pl.pallas_call(
        kernel,
        out_shape=[jax.ShapeDtypeStruct(*s) for s in shapes],
        in_specs=[pl.BlockSpec(memory_space=space) for space in spaces],
        out_specs=[pl.BlockSpec(memory_space=pltpu.VMEM)] * len(shapes),
        scratch_shapes=list(scratch),
        compiler_params=pltpu.CompilerParams(vmem_limit_bytes=VMEM_LIMIT),
        cost_estimate=cost,
    )(*operands)
    return result[0] if single else result


def exchange(x, groups):
    return lax.all_gather(x, "seq", axis_index_groups=groups)


def near(*offsets):
    groups, taken = [], set()
    for i in range(PARTS):
        if i not in taken:
            groups.append([i + offset for offset in offsets])
            taken.update(groups[-1])
    return groups


def hop(x, place):
    up = [(8 * place + i, 8 * place + i + 8) for i in range(0, 8, 2)]
    return lax.ppermute(x, "seq", up + [(PARTS - 1 - a, PARTS - 1 - b) for a, b in up])


def shards(queries, raw_keys, values, cotangent):
    index = (lax.axis_index("seq") + PARTS * lax.axis_index("head")).astype(jnp.int32).reshape(1)
    q = queries.reshape(2 * T, D)
    v = values.reshape(2 * T, D)
    d = cotangent.reshape(2 * T, D)
    wide = pltpu.VMEM((2 * T, D), F32)
    key, norm, inv = call(
        keys_kernel, [((T, D), F32), ((T, D), F32), ((T, T), F32)], raw_keys, scalars=0, cost=LONG
    )
    send, w, x0 = call(
        before_kernel,
        [((D, 5 * D), F32), ((T, D), F32), ((T, 2 * D), F32)],
        index, key, inv, q, v, d,
        scratch=[wide] * 3,
    )
    pair = exchange(send, near(0, 1))
    own, send = call(pair_kernel, [((D, 2 * D), F32)] * 2, index, pair)
    chip, send = call(chip_kernel, [((D, 2 * D), F32)] * 2, index, own, exchange(send, near(0, 2)))
    units = exchange(send, near(0, 4))
    send, block = call(block_kernel, [((D, D), F32), ((D, 2 * D), F32)], index, units)
    first = hop(send, 0)
    m, z0 = call(
        side_kernel,
        [((T, D), F32), ((T, 2 * D), F32)],
        index, send, key, inv, q, d,
        scratch=[wide] * 2,
        cost=SHORT,
    )
    send = call(hop_kernel, ((D, D), F32), first, block, scalars=0)
    second = hop(send, 1)
    send = call(hop_kernel, ((D, D), F32), second, block, scalars=0)
    third = hop(send, 2)
    send = call(top_kernel, ((D, 2 * D), F32), index, first, second, third, units, chip)
    got = exchange(send, near(0, 1, 2, 3))
    gk, state, x, z = call(
        after_kernel,
        [((T, D), F32), ((D, 2 * D), F32), ((T, 2 * D), F32), ((T, 2 * D), F32)],
        index, pair, got, q, d, key, w, m, x0, z0,
        scratch=[wide] * 2,
    )
    peers = lax.axis_size("head")
    pieces = lax.all_to_all(gk.reshape(peers, T // peers, D), "head", 0, 0)
    out, gq, gv = call(
        rest_kernel,
        [((2 * T, D), BF16)] * 3,
        index, q, d, key, state, x, z,
        scratch=[wide] * 5,
        cost=LONG,
    )
    totals = call(sum_kernel, ((peers, T // peers, D), F32), index, pieces, key, norm)
    total = lax.all_to_all(totals, "head", 0, 0).reshape(T, D)
    gkey = call(key_kernel, ((T, D), BF16), total, scalars=0)
    shape = queries.shape
    return out.reshape(shape), gq.reshape(shape), gkey, gv.reshape(shape)


def solution(mesh):
    split_both = P("seq", "head", None)
    keys_only = P("seq", None)
    return jax.shard_map(
        shards,
        mesh=mesh,
        in_specs=(split_both, keys_only, split_both, split_both),
        out_specs=(split_both, split_both, keys_only, split_both),
        check_vma=False,
    )
```
